256 devices in a mesh: expert: 32 (over y, x, core), rep: 8 (over z).
Axes of the slice: x: 4, y: 4, z: 8, core: 2. Of those that a mesh axis runs over, the one named last changes fastest.
Arguments:
- node_feats: bfloat16 [8, 8192, 768], P('rep', 'expert'), may hold values from -32 to 32
- edge_src: int32 [8, 32768], P('rep', 'expert'), may hold values from 0 to 383, as said below
- edge_dst: int32 [8, 32768], P('rep', 'expert'), may hold values from -1 to 255, as said below
- node_codes: int32 [8, 8192, 1], P('rep', 'expert'), may hold values from 0 to 31, as said below
- norm_gain: float32 [768], replicated, may hold values from 0.1 to 1.9
- w_gate: bfloat16 [32, 768, 1536], P('expert'), may hold values from -0.21875 to 0.21875
- w_up: bfloat16 [32, 768, 1536], P('expert'), may hold values from -0.21875 to 0.21875
- w_down_t: bfloat16 [32, 768, 1536], P('expert'), may hold values from -0.15625 to 0.15625
- d_out: bfloat16 [8, 8192, 768], P('rep', 'expert'), may hold values from -6 to 6
Outputs:
- layer_out: bfloat16 [8, 8192, 768], P('rep', 'expert')
- d_node_feats: bfloat16 [8, 8192, 768], P('rep', 'expert')
- grad_w_gate: float32 [32, 768, 1536], P('expert', None, 'rep')
- grad_w_up: float32 [32, 768, 1536], P('expert', None, 'rep')
- grad_w_down_t: float32 [32, 768, 1536], P('expert', None, 'rep')
The draws below stay inside these ranges and needn't reach their ends.
Inputs may be any that keep to these rules, and one draw needn't show every extreme that they name: `node_codes`: within each partition (256 consecutive nodes of a graph) at most 16 nodes carry one code; one code, the same for all partitions of a draw, is carried by exactly 16 nodes of every partition. `edge_src`: A row of the partition's extended rows: the last 64 nodes of the previous partition, then its own 256 nodes, then the first 64 nodes of the next partition. `edge_dst`: A node's position within the partition, or -1 for a padding slot; a partition's padding slots are the last of its 1024 slots, at least one.
All inputs are finite; a program needn't handle non-finite values.
Results may differ from the reference program's by a relative error of at most 0.015.
Values may be sent and summed in bfloat16 or wider, within the bound.
A program may use at most 128 MiB of HBM per device.

```python
import math
from functools import partial
import jax
import jax.numpy as jnp
from jax import lax

D = 768
FF = 1536
NODE_DEV = 256
BND = 64
EDGE_DEV = 1024
EXPERTS = 32
GN = 8192
CAP = 16
N_EXPERT = 32
N_REP = 8


def draw_node_feats(key, part):
    key = jax.random.fold_in(key, 11)
    base_key, column_key, row_key = jax.random.split(key, 3)
    shape = (N_REP, N_EXPERT * NODE_DEV, D)
    column_scale = jnp.exp(jax.random.uniform(column_key, (D,), jnp.float32, math.log(0.4), math.log(4.0)))
    row_scale = jnp.exp(jax.random.uniform(row_key, (N_REP, N_EXPERT * NODE_DEV, 1), jnp.float32, math.log(0.5), math.log(2.0)))
    base_draw = jnp.clip(jax.random.normal(base_key, shape, jnp.float32), -4.0, 4.0)
    return (base_draw * column_scale * row_scale).astype(jnp.bfloat16)


def draw_edge_src(key, part):
    key = jax.random.fold_in(key, 37)
    extent = NODE_DEV + 2 * BND
    values = jax.random.randint(key, (N_REP, N_EXPERT * EDGE_DEV), 0, extent)
    return values.astype(jnp.int32)


def draw_edge_dst(key, part):
    key = jax.random.fold_in(key, 41)
    value_key, count_key = jax.random.split(key)
    values = jax.random.randint(value_key, (N_REP, N_EXPERT, EDGE_DEV), 0, NODE_DEV)
    live_count = jax.random.randint(count_key, (N_REP, N_EXPERT, 1), 5 * EDGE_DEV // 8, EDGE_DEV)
    position = jnp.arange(EDGE_DEV, dtype=jnp.int32)[None, None, :]
    values = jnp.where(position < live_count, values, -1)
    return values.reshape(N_REP, N_EXPERT * EDGE_DEV).astype(jnp.int32)


def draw_node_codes(key, part):
    key = jax.random.fold_in(key, 23)
    hot_key, spread_key, block_key = jax.random.split(key, 3)
    block_total = N_REP * N_EXPERT
    hot_code = jax.random.randint(hot_key, (), 0, EXPERTS)
    lowest = max((EXPERTS - 1) // 2, 1)
    spread = jax.random.randint(spread_key, (block_total,), lowest, EXPERTS)

    def one_block(block_seed, subset_size):
        order_key, place_key = jax.random.split(block_seed)
        others = jax.random.permutation(order_key, EXPERTS - 1)
        counter = jnp.arange(NODE_DEV - CAP, dtype=jnp.int32)
        chosen = others[counter % subset_size]
        chosen = chosen + (chosen >= hot_code).astype(jnp.int32)
        sequence = jnp.concatenate([jnp.full((CAP,), hot_code, jnp.int32), chosen.astype(jnp.int32)])
        return jax.random.permutation(place_key, sequence)
    block_keys = jax.random.split(block_key, block_total)
    codes_all = jax.vmap(one_block)(block_keys, spread)
    return codes_all.reshape(N_REP, N_EXPERT * NODE_DEV, 1).astype(jnp.int32)


def steps_of(key, shape, cuts, smallest, largest):
    level, own = 1.0, jax.random.fold_in(key, 6)
    for axis_at, shards_of in cuts:
        steps = jnp.exp(jax.random.uniform(jax.random.fold_in(own, axis_at), (shards_of,), jnp.float32, smallest / len(cuts), largest / len(cuts)))
        level = level * jnp.repeat(steps, shape[axis_at] // shards_of).reshape([-1 if axis == axis_at else 1 for axis in range(len(shape))])
    return level


def gaussian(key, shape, deviation, most, pieces=(), kind=jnp.bfloat16):
    entries = jax.random.normal(key, shape, jnp.float32) * deviation
    if len(pieces) > 0:
        entries = steps_of(key, shape, pieces, -0.22, 0.18) * entries
    return jnp.clip(entries, min=-most, max=most).astype(kind)


def setup_inputs(seed: int = 0) -> dict:
    keys = jax.random.split(jax.random.key(seed), 10)
    return {
        "node_feats": draw_node_feats(jax.random.fold_in(keys[9], 71), 0),
        "edge_src": draw_edge_src(jax.random.fold_in(keys[9], 71), 0),
        "edge_dst": draw_edge_dst(jax.random.fold_in(keys[9], 71), 0),
        "node_codes": draw_node_codes(jax.random.fold_in(keys[9], 71), 0),
        "norm_gain": jnp.clip(1.0 + 0.18 * jax.random.normal(keys[4], (D,), jnp.float32), 0.1, 1.9),
        "w_gate": gaussian(keys[5], (EXPERTS, D, FF), D ** -0.5, 0.21875, ((0, 32),)),
        "w_up": gaussian(keys[6], (EXPERTS, D, FF), D ** -0.5, 0.21875, ((0, 32),)),
        "w_down_t": gaussian(keys[7], (EXPERTS, D, FF), FF ** -0.5, 0.15625, ((0, 32),)),
        "d_out": gaussian(keys[8], (N_REP, GN, D), 1.0, 6.0, ((0, 8), (1, 32))),
    }


def edge_index(source_ids, target_ids):
    extent = NODE_DEV + 2 * BND
    offsets = jnp.arange(N_EXPERT, dtype=jnp.int32)[:, None]
    source_flat = (offsets * extent + source_ids.reshape(N_EXPERT, EDGE_DEV).astype(jnp.int32)).reshape(-1)
    target_block = target_ids.reshape(N_EXPERT, EDGE_DEV).astype(jnp.int32)
    target_flat = jnp.where(target_block >= 0, offsets * NODE_DEV + target_block, N_EXPERT * NODE_DEV)
    return (source_flat.astype(jnp.int32), target_flat.reshape(-1).astype(jnp.int32))

def graph_forward(operands, norm_gain):
    node_block, source_ids, target_ids = operands
    node_total = N_EXPERT * NODE_DEV
    extent = NODE_DEV + 2 * BND
    blocks = node_block.reshape(N_EXPERT, NODE_DEV, D)
    extended = jnp.concatenate([jnp.roll(blocks, 1, 0)[:, NODE_DEV - BND:], blocks, jnp.roll(blocks, -1, 0)[:, :BND]], 1)
    extended = extended.reshape(N_EXPERT * extent, D)
    source_flat, target_flat = edge_index(source_ids, target_ids)
    message = extended[source_flat].astype(jnp.float32)
    summed = jax.ops.segment_sum(message, target_flat, node_total + 1)[:node_total]
    degree = jax.ops.segment_sum(jnp.ones(target_flat.shape, jnp.float32), target_flat, node_total + 1)[:node_total]
    inverse = 1.0 / jnp.maximum(degree, 1.0)
    mixed_rows = node_block.astype(jnp.float32) + summed * inverse[:, None]
    scaling = lax.rsqrt(lax.optimization_barrier(jnp.mean(mixed_rows * mixed_rows, axis=1, keepdims=True)) + 1e-05)
    normal = mixed_rows * scaling
    routed = (normal * norm_gain[None, :]).astype(jnp.bfloat16)
    return (routed, normal, scaling, inverse)

def graph_backward(operands, norm_gain):
    d_routed, normal, scaling, inverse, source_ids, target_ids, d_block = operands
    extent = NODE_DEV + 2 * BND
    d_norm = d_routed.astype(jnp.float32) * norm_gain[None, :]
    d_mixed = scaling * (d_norm - normal * lax.optimization_barrier(jnp.mean(d_norm * normal, axis=1, keepdims=True)))
    d_mean = (d_mixed * inverse[:, None]).astype(jnp.bfloat16)
    source_flat, target_flat = edge_index(source_ids, target_ids)
    padded_mean = jnp.concatenate([d_mean, jnp.zeros((1, D), jnp.bfloat16)], 0)
    d_message = padded_mean[target_flat].astype(jnp.float32)
    d_extended = jax.ops.segment_sum(d_message, source_flat, N_EXPERT * extent).reshape(N_EXPERT, extent, D)
    inner = d_extended[:, BND:BND + NODE_DEV]
    inner = inner.at[:, :BND].add(jnp.roll(d_extended[:, BND + NODE_DEV:], 1, 0))
    inner = inner.at[:, NODE_DEV - BND:].add(jnp.roll(d_extended[:, :BND], -1, 0))
    total_grad = d_block.astype(jnp.float32) + d_mixed + inner.reshape(N_EXPERT * NODE_DEV, D)
    return total_grad.astype(jnp.bfloat16)

def replica_sum(left, right):
    right_rows = right.reshape(left.shape[0], left.shape[1], right.shape[-1])
    per_graph = jnp.einsum('rmd,rmf->rdf', left.astype(jnp.float32), right_rows.astype(jnp.float32))
    rounded = lax.optimization_barrier(per_graph.astype(jnp.bfloat16))
    return lax.optimization_barrier(jnp.sum(rounded.astype(jnp.float32), axis=0))

def expert_pass(operands):
    rows_in, grads_in, gate_weight, up_weight, down_weight = operands
    flat_rows = rows_in.reshape(-1, D)
    flat_grads = grads_in.reshape(-1, D)
    gate_pre = jnp.dot(flat_rows, gate_weight, preferred_element_type=jnp.float32)
    up_pre = jnp.dot(flat_rows, up_weight, preferred_element_type=jnp.float32)
    sigmoid_gate = jax.nn.sigmoid(gate_pre)
    silu_gate = gate_pre * sigmoid_gate
    hidden = (silu_gate * up_pre).astype(jnp.bfloat16)
    expert_out = lax.dot_general(hidden, down_weight, (((1,), (1,)), ((), ())), preferred_element_type=jnp.float32).astype(jnp.bfloat16)
    back_hidden = jnp.dot(flat_grads, down_weight, preferred_element_type=jnp.float32)
    d_gate = (back_hidden * up_pre * sigmoid_gate * (1.0 + gate_pre * (1.0 - sigmoid_gate))).astype(jnp.bfloat16)
    d_up = (back_hidden * silu_gate).astype(jnp.bfloat16)
    d_routed = lax.dot_general(d_gate, gate_weight, (((1,), (1,)), ((), ())), preferred_element_type=jnp.float32)
    d_routed = d_routed + lax.dot_general(d_up, up_weight, (((1,), (1,)), ((), ())), preferred_element_type=jnp.float32)
    d_routed = d_routed.astype(jnp.bfloat16)
    grad_gate = replica_sum(rows_in, d_gate)
    grad_up = replica_sum(rows_in, d_up)
    grad_down = replica_sum(grads_in, hidden)
    return (expert_out.reshape(rows_in.shape), d_routed.reshape(rows_in.shape), grad_gate, grad_up, grad_down)

def reference(node_feats, edge_src, edge_dst, node_codes, norm_gain, w_gate, w_up, w_down_t, d_out):
    routed, normal, scaling, inverse = lax.map(partial(graph_forward, norm_gain=norm_gain), (node_feats, edge_src, edge_dst))
    expert_ids = node_codes[:, :, 0].reshape(N_REP, N_EXPERT, NODE_DEV).astype(jnp.int32)
    member = (expert_ids[..., None] == jnp.arange(EXPERTS, dtype=jnp.int32)).astype(jnp.int32)
    slot_ids = lax.optimization_barrier(jnp.sum((jnp.cumsum(member, axis=2) - member) * member, axis=3)).astype(jnp.int32)
    bucket_pos = (jnp.arange(N_EXPERT, dtype=jnp.int32)[None, :, None] * CAP + slot_ids).astype(jnp.int32)
    graph_ids = jnp.broadcast_to(jnp.arange(N_REP, dtype=jnp.int32)[:, None, None], expert_ids.shape)
    empty = jnp.zeros((EXPERTS, N_REP, N_EXPERT * CAP, D), jnp.bfloat16)
    bucket_rows = empty.at[expert_ids, graph_ids, bucket_pos].set(routed.reshape(N_REP, N_EXPERT, NODE_DEV, D))
    bucket_grads = empty.at[expert_ids, graph_ids, bucket_pos].set(d_out.reshape(N_REP, N_EXPERT, NODE_DEV, D))
    expert_out, d_bucket, grad_gate, grad_up, grad_down = lax.map(expert_pass, (bucket_rows, bucket_grads, w_gate, w_up, w_down_t))
    node_out = expert_out[expert_ids, graph_ids, bucket_pos].reshape(N_REP, N_EXPERT * NODE_DEV, D)
    layer_out = (node_feats.astype(jnp.float32) + node_out.astype(jnp.float32)).astype(jnp.bfloat16)
    d_routed = d_bucket[expert_ids, graph_ids, bucket_pos].reshape(N_REP, N_EXPERT * NODE_DEV, D)
    d_node_feats = lax.map(partial(graph_backward, norm_gain=norm_gain), (d_routed, normal, scaling, inverse, edge_src, edge_dst, d_out))
    return (layer_out, d_node_feats, grad_gate, grad_up, grad_down)
```

```python
import jax
import jax.numpy as jnp
from jax import lax
from jax.experimental import pallas as pl
from jax.experimental.pallas import tpu as pltpu
from jax.sharding import PartitionSpec as P

MESH = pl.DeviceIdType.MESH
F32 = jnp.float32
BF16 = jnp.bfloat16

D = 768
FF = 1536
NODES = 256
RIM = 64
EXTENT = NODES + 2 * RIM
EDGES = 1024
EXPERTS = 32
CAP = 16
ROWS = EXPERTS * CAP
REPS = 8
SLICE = FF // REPS
HALF = D // 2


def partner_order():
    hops = (0, 1, 2, 1)
    offsets = [(a, b, c) for a in range(4) for b in range(4) for c in range(2)][1:]
    offsets.sort(key=lambda o: -(hops[o[0]] + hops[o[1]]))
    order = []
    for o in offsets:
        opposite = ((4 - o[0]) % 4, (4 - o[1]) % 4, o[2])
        for p in (o, opposite):
            if p not in order:
                order.append(p)
    return order


ORDER = partner_order()


def dot(a, b):
    return jnp.dot(a, b, preferred_element_type=F32)


def dot_last(a, b):
    return lax.dot_general(a, b, (((1,), (1,)), ((), ())), preferred_element_type=F32)


def chunk(i, size):
    return pl.ds(pl.multiple_of(i * size, size), size)


def kernel(
    nodes, sources, targets, codes, gain, w_gate, w_up, w_down, d_out,
    layer_out, d_nodes, grad_gate, grad_up, grad_down,
    wg, wu, wd, wgt, wut, wdt, partial, ring,
    send_g, send_r, recv_g, recv_r, back_e, back_d, ret_e, ret_d,
    hid_t, dgate_t, dup_t, bh_t, gate_s, up_s,
    normal, total, counts, counts_t, place, place_t, scale_s, inv_s,
    rim_in, rim_out, rim_back, dmean,
    w_sem, rim_send, rim_recv, a2a_send, a2a_recv, ring_send, ring_recv,
):
    me = lax.axis_index("expert")
    rep = lax.axis_index("rep")
    my, mx, mc = me // 8, lax.rem(me // 2, 4), lax.rem(me, 2)
    following, before = lax.rem(me + 1, EXPERTS), lax.rem(me + EXPERTS - 1, EXPERTS)
    rep_up, rep_down = lax.rem(rep + 1, REPS), lax.rem(rep + REPS - 1, REPS)

    def partner(offset):
        a, b, c = offset
        return lax.rem(my + a, 4) * 8 + lax.rem(mx + b, 4) * 2 + lax.rem(mc + c, 2)

    barrier = pltpu.get_barrier_semaphore()

    def greet(i, carry):
        pl.semaphore_signal(
            barrier, inc=1, device_id=(lax.rem(me + i, EXPERTS), rep), device_id_type=MESH
        )
        return carry

    lax.fori_loop(1, EXPERTS, greet, 0)
    for z in (rep_up, rep_down):
        pl.semaphore_signal(barrier, inc=1, device_id=(me, z), device_id_type=MESH)

    loads = [
        pltpu.make_async_copy(src, dst, w_sem.at[i])
        for i, (src, dst) in enumerate(((w_down, wd), (w_gate, wg), (w_up, wu)))
    ]
    for load in loads:
        load.start()

    code_row = codes[...].astype(F32)
    code_col = jnp.transpose(jnp.broadcast_to(code_row, (128, NODES)))[:, :1]
    first = lax.broadcasted_iota(jnp.int32, (NODES, NODES), 0)
    second = lax.broadcasted_iota(jnp.int32, (NODES, NODES), 1)
    same = code_col == code_row
    rank_row = jnp.sum(jnp.where(same & (first < second), 1.0, 0.0), axis=0, keepdims=True)
    rank_col = jnp.sum(jnp.where(same & (second < first), 1.0, 0.0), axis=1, keepdims=True)
    slot_row = (code_row * CAP + rank_row).astype(jnp.int32)
    slot_col = (code_col * CAP + rank_col).astype(jnp.int32)
    place_t[...] = jnp.where(
        lax.broadcasted_iota(jnp.int32, (ROWS, NODES), 0) == slot_row, 1.0, 0.0
    ).astype(BF16)
    place[...] = jnp.where(
        lax.broadcasted_iota(jnp.int32, (NODES, ROWS), 1) == slot_col, 1.0, 0.0
    ).astype(BF16)

    def bucket(rows, out):
        out[...] = dot(place_t[...], rows[...]).astype(BF16).reshape(EXPERTS, CAP, D)

    bucket(d_out, send_g)

    src = sources[...]
    src = jnp.where(src >= RIM, src - RIM, src + (EXTENT - RIM))
    source_hot = jnp.where(
        lax.broadcasted_iota(jnp.int32, (EXTENT, EDGES), 0) == src, 1.0, 0.0
    ).astype(BF16)
    target_hot = jnp.where(
        lax.broadcasted_iota(jnp.int32, (NODES, EDGES), 0) == targets[...], 1.0, 0.0
    ).astype(BF16)
    count = dot_last(target_hot, source_hot)
    counts[...] = count.astype(BF16)
    counts_t[...] = jnp.transpose(count).astype(BF16)
    inv_s[...] = 1.0 / jnp.maximum(jnp.sum(count, axis=1, keepdims=True), 1.0)

    pl.semaphore_wait(barrier, EXPERTS + 1)

    def rim_copies(low, high, landing, base):
        return [
            pltpu.make_async_remote_copy(
                low, landing.at[pl.ds(0, RIM)], rim_send.at[base], rim_recv.at[base],
                device_id=(before, rep), device_id_type=MESH,
            ),
            pltpu.make_async_remote_copy(
                high, landing.at[pl.ds(RIM, RIM)], rim_send.at[base + 1], rim_recv.at[base + 1],
                device_id=(following, rep), device_id_type=MESH,
            ),
        ]

    rim_first = rim_copies(nodes.at[pl.ds(0, RIM)], nodes.at[pl.ds(NODES - RIM, RIM)], rim_in, 0)
    for copy in rim_first:
        copy.start()

    def exchange(source, landing, slot):
        for offset in ORDER:
            t = partner(offset)
            pltpu.make_async_remote_copy(
                source.at[t], landing.at[me], a2a_send.at[slot], a2a_recv.at[slot],
                device_id=(t, rep), device_id_type=MESH,
            ).start()
        landing[me] = source[me]

    def exchange_wait(landing, slot):
        part = landing.at[pl.ds(0, EXPERTS - 1)]
        pltpu.make_async_copy(part, part, a2a_recv.at[slot]).wait()

    def exchange_sent(source, slot):
        part = source.at[pl.ds(0, EXPERTS - 1)]
        pltpu.make_async_copy(part, part, a2a_send.at[slot]).wait()

    exchange(send_g, recv_g, 0)

    total[...] = dot(counts[:, pl.ds(0, NODES)], nodes[...])
    for copy in rim_first:
        copy.wait_recv()
    total[...] += dot(counts[:, pl.ds(NODES, 2 * RIM)], rim_in[...])

    def normalize(i, carry):
        at = chunk(i, 32)
        mixed = nodes[at, :].astype(F32) + total[at, :] * inv_s[at, :]
        scaling = lax.rsqrt(jnp.mean(mixed * mixed, axis=1, keepdims=True) + 1e-05)
        scale_s[at, :] = scaling
        norm = mixed * scaling
        normal[at, :] = norm
        dmean[at, :] = (norm * gain[...]).astype(BF16)
        return carry

    lax.fori_loop(0, NODES // 32, normalize, 0)
    bucket(dmean, send_r)
    exchange(send_r, recv_r, 1)

    def turn(source, out):
        def body(i, carry):
            out[chunk(i, 128), :] = jnp.transpose(source[:, chunk(i, 128)])
            return carry

        lax.fori_loop(0, FF // 128, body, 0)

    loads[0].wait()
    turn(wd, wdt)
    loads[1].wait()
    turn(wg, wgt)
    loads[2].wait()
    turn(wu, wut)

    exchange_wait(recv_g, 0)

    def flat(ref):
        return ref[...].reshape(ROWS, D)

    def back(i, carry):
        at = chunk(i, SLICE)
        bh_t[at, :] = dot_last(wdt[at, :], flat(recv_g))
        return carry

    lax.fori_loop(0, REPS, back, 0)
    exchange_wait(recv_r, 1)

    def expert_slice(c):
        base = pl.multiple_of(c * SLICE, SLICE)
        at = pl.ds(base, SLICE)
        gate_s[...] = dot_last(wgt[at, :], flat(recv_r))
        up_s[...] = dot_last(wut[at, :], flat(recv_r))

        def act(i, carry):
            rows = chunk(i, 16)
            here = pl.ds(pl.multiple_of(base + i * 16, 16), 16)
            g, u, b = gate_s[rows, :], up_s[rows, :], bh_t[here, :]
            s = jax.nn.sigmoid(g)
            silu = g * s
            hid_t[here, :] = (silu * u).astype(BF16)
            dgate_t[here, :] = (b * u * s * (1.0 + g * (1.0 - s))).astype(BF16)
            dup_t[here, :] = (b * silu).astype(BF16)
            return carry

        lax.fori_loop(0, SLICE // 16, act, 0)
        for j, (left, right) in enumerate(
            ((hid_t, recv_g), (dgate_t, recv_r), (dup_t, recv_r))
        ):
            g = dot(left[at, :], flat(right)).astype(BF16)
            partial[c, j, 0] = g[:, :HALF]
            partial[c, j, 1] = g[:, HALF:]

    def mod(i):
        return lax.rem(i + 2 * REPS, REPS)

    def piece(d, k):
        return mod(rep - 1 - k) if d == 0 else mod(rep + 1 + k)

    def hop(d, k, j):
        source = partial.at[piece(d, 0), j, d] if k == 0 else ring.at[k - 1, j, d]
        return pltpu.make_async_remote_copy(
            source, ring.at[k, j, d], ring_send.at[k, j, d], ring_recv.at[k, j, d],
            device_id=(me, rep_up if d == 0 else rep_down), device_id_type=MESH,
        )

    def serve(k, j):
        for d in range(2):
            hop(d, k - 1, j).wait_recv()
            c = piece(d, k)

            def add(i, carry):
                at = chunk(i, 32)
                ring[k - 1, j, d, at, :] = (
                    ring[k - 1, j, d, at, :].astype(F32) + partial[c, j, d, at, :].astype(F32)
                ).astype(BF16)
                return carry

            lax.fori_loop(0, SLICE // 32, add, 0)
            hop(d, k, j).start()

    def pair(i):
        other = mod(rep + 1 + i) if i < 3 else rep

        def body(s, carry):
            expert_slice(jnp.where(s == 0, mod(rep - 1 - i), other))
            return carry

        lax.fori_loop(0, 2, body, 0)

    pair(0)
    for j in range(3):
        for d in range(2):
            hop(d, 0, j).start()
    pair(1)
    serve(1, 0)
    pair(2)
    serve(1, 1)
    pair(3)
    serve(1, 2)

    def project(terms, out):
        def body(b, carry):
            at = chunk(b, 256)
            y = dot(terms[0][0][at, :], terms[0][1][...])
            for w, x in terms[1:]:
                y = y + dot(w[at, :], x[...])
            out[:, :, at] = jnp.transpose(y).astype(BF16).reshape(EXPERTS, CAP, 256)
            return carry

        lax.fori_loop(0, D // 256, body, 0)

    project(((wd, hid_t),), back_e)
    exchange(back_e, ret_e, 2)
    serve(2, 0)
    project(((wg, dgate_t), (wu, dup_t)), back_d)
    exchange(back_d, ret_d, 3)
    serve(2, 1)
    serve(2, 2)
    for j in range(3):
        serve(3, j)
    for j in range(3):
        serve(4, j)

    exchange_wait(ret_e, 2)
    total[...] = dot(place[...], flat(ret_e))

    def forward_out(i, carry):
        at = chunk(i, 32)
        layer_out[at, :] = (nodes[at, :].astype(F32) + total[at, :]).astype(BF16)
        return carry

    lax.fori_loop(0, NODES // 32, forward_out, 0)
    exchange_wait(ret_d, 3)
    total[...] = dot(place[...], flat(ret_d))
    serve(5, 0)

    def norm_back(i, carry):
        at = chunk(i, 32)
        d_norm = total[at, :] * gain[...]
        norm = normal[at, :]
        d_mixed = scale_s[at, :] * (d_norm - norm * jnp.mean(d_norm * norm, axis=1, keepdims=True))
        dmean[at, :] = (d_mixed * inv_s[at, :]).astype(BF16)
        total[at, :] = d_out[at, :].astype(F32) + d_mixed
        return carry

    lax.fori_loop(0, NODES // 32, norm_back, 0)
    rim_out[...] = dot(counts_t[pl.ds(NODES, 2 * RIM), :], dmean[...]).astype(BF16)
    rim_last = rim_copies(rim_out.at[pl.ds(RIM, RIM)], rim_out.at[pl.ds(0, RIM)], rim_back, 2)
    for copy in rim_last:
        copy.start()
    serve(5, 1)
    total[...] += dot(counts_t[pl.ds(0, NODES), :], dmean[...])
    serve(5, 2)
    for copy in rim_last:
        copy.wait_recv()
    total[pl.ds(0, RIM), :] += rim_back[pl.ds(RIM, RIM), :].astype(F32)
    total[pl.ds(NODES - RIM, RIM), :] += rim_back[pl.ds(0, RIM), :].astype(F32)
    serve(6, 0)

    def node_out(i, carry):
        at = chunk(i, 32)
        d_nodes[at, :] = total[at, :].astype(BF16)
        return carry

    lax.fori_loop(0, NODES // 32, node_out, 0)
    serve(6, 1)
    serve(6, 2)
    for j, out in enumerate((grad_down, grad_gate, grad_up)):
        for d in range(2):
            hop(d, 6, j).wait_recv()
            y = ring[6, j, d].astype(F32) + partial[rep, j, d].astype(F32)
            out[pl.ds(d * HALF, HALF), :] = jnp.transpose(y)

    for copy in rim_first + rim_last:
        copy.wait_send()
    for slot, source in enumerate((send_g, send_r, back_e, back_d)):
        exchange_sent(source, slot)
    for k in range(REPS - 1):
        for j in range(3):
            for d in range(2):
                hop(d, k, j).wait_send()


def on_device(node_feats, edge_src, edge_dst, node_codes, norm_gain, w_gate, w_up, w_down_t, d_out):
    vmem, hbm = pl.BlockSpec(memory_space=pltpu.VMEM), pl.BlockSpec(memory_space=pl.ANY)
    weight = pltpu.VMEM((D, FF), BF16)
    weight_t = pltpu.VMEM((FF, D), BF16)
    buckets = pltpu.VMEM((EXPERTS, CAP, D), BF16)
    act_t = pltpu.VMEM((FF, ROWS), BF16)
    rims = pltpu.VMEM((2 * RIM, D), BF16)
    sem = pltpu.SemaphoreType.DMA
    out = pl.pallas_call(
        kernel,
        out_shape=[jax.ShapeDtypeStruct((NODES, D), BF16)] * 2
        + [jax.ShapeDtypeStruct((D, SLICE), F32)] * 3,
        in_specs=[vmem] * 5 + [hbm] * 3 + [vmem],
        out_specs=[vmem] * 5,
        scratch_shapes=[weight] * 3
        + [weight_t] * 3
        + [
            pltpu.VMEM((REPS, 3, 2, SLICE, HALF), BF16),
            pltpu.VMEM((REPS - 1, 3, 2, SLICE, HALF), BF16),
        ]
        + [buckets] * 8
        + [act_t] * 3
        + [
            pltpu.VMEM((FF, ROWS), F32),
            pltpu.VMEM((SLICE, ROWS), F32),
            pltpu.VMEM((SLICE, ROWS), F32),
            pltpu.VMEM((NODES, D), F32),
            pltpu.VMEM((NODES, D), F32),
            pltpu.VMEM((NODES, EXTENT), BF16),
            pltpu.VMEM((EXTENT, NODES), BF16),
            pltpu.VMEM((NODES, ROWS), BF16),
            pltpu.VMEM((ROWS, NODES), BF16),
            pltpu.VMEM((NODES, 1), F32),
            pltpu.VMEM((NODES, 1), F32),
        ]
        + [rims] * 3
        + [
            pltpu.VMEM((NODES, D), BF16),
            sem((3,)),
            sem((4,)),
            sem((4,)),
            sem((4,)),
            sem((4,)),
            sem((REPS - 1, 3, 2)),
            sem((REPS - 1, 3, 2)),
        ],
        compiler_params=pltpu.CompilerParams(
            collective_id=0, has_side_effects=True, vmem_limit_bytes=60 * 2**20
        ),
        name="graph_moe",
    )(
        node_feats[0], edge_src, edge_dst, node_codes.reshape(1, NODES), norm_gain.reshape(1, D),
        w_gate[0], w_up[0], w_down_t[0], d_out[0],
    )
    return tuple(x[None] for x in out)


def solution(mesh):
    rows = P("rep", "expert", None)
    edges = P("rep", "expert")
    weights = P("expert", None, None)
    grads = P("expert", None, "rep")
    return jax.shard_map(
        on_device,
        mesh=mesh,
        in_specs=(rows, edges, edges, rows, P(), weights, weights, weights, rows),
        out_specs=(rows, rows, grads, grads, grads),
        check_vma=False,
    )
```

```python
import jax
import jax.numpy as jnp
from jax import lax
from jax.experimental import pallas as pl
from jax.experimental.pallas import tpu as pltpu
from jax.sharding import PartitionSpec as P

MESH = pl.DeviceIdType.MESH
F32 = jnp.float32
BF16 = jnp.bfloat16

D = 768
FF = 1536
NODES = 256
RIM = 64
EXTENT = NODES + 2 * RIM
EDGES = 1024
EXPERTS = 32
CAP = 16
ROWS = EXPERTS * CAP
REPS = 8
SLICE = FF // REPS
PART = SLICE // 2


def partner_order():
    hops = (0, 1, 2, 1)
    offsets = [(a, b) for a in range(4) for b in range(4)][1:]
    offsets.sort(key=lambda o: -(hops[o[0]] + hops[o[1]]))
    order = []
    for a, b in offsets:
        for p in ((a, b), ((4 - a) % 4, (4 - b) % 4)):
            if p not in order:
                order.append(p)
    return order


ORDER = partner_order()
CHIPS = len(ORDER)


def dot(a, b):
    return jnp.dot(a, b, preferred_element_type=F32)


def dot_last(a, b):
    return lax.dot_general(a, b, (((1,), (1,)), ((), ())), preferred_element_type=F32)


def chunk(i, size):
    return pl.ds(pl.multiple_of(i * size, size), size)


def kernel(
    nodes_hbm, sources_hbm, targets_hbm, codes_hbm, gain_hbm, w_gate, w_up, w_down, d_out_hbm,
    layer_out, d_nodes, grad_gate, grad_up, grad_down,
    nodes, sources, targets, codes, gain, d_out,
    wg, wu, wd, wgt, wut, wdt, partial, ring,
    send_g, send_r, recv_g, recv_r, back_e, back_d, ret_e, ret_d,
    hid_t, dgate_t, dup_t, bh_s, gate_s, up_s,
    normal, total, counts, counts_t, place, place_t, scale_s, inv_s,
    rim_in, rim_out, rim_back, dmean,
    load_sem, rim_send, rim_recv, a2a_send, a2a_recv, ring_send, ring_recv,
):
    me = lax.axis_index("expert")
    rep = lax.axis_index("rep")
    my, mx, mc = me // 8, lax.rem(me // 2, 4), lax.rem(me, 2)
    following, before = lax.rem(me + 1, EXPERTS), lax.rem(me + EXPERTS - 1, EXPERTS)
    rep_up, rep_down = lax.rem(rep + 1, REPS), lax.rem(rep + REPS - 1, REPS)

    barrier = pltpu.get_barrier_semaphore()

    def greet(i, carry):
        pl.semaphore_signal(
            barrier, inc=1, device_id=(lax.rem(me + i, EXPERTS), rep), device_id_type=MESH
        )
        return carry

    lax.fori_loop(1, EXPERTS, greet, 0)
    for z in (rep_up, rep_down):
        pl.semaphore_signal(barrier, inc=1, device_id=(me, z), device_id_type=MESH)

    pairs = (
        (codes_hbm, codes), (d_out_hbm, d_out), (sources_hbm, sources), (targets_hbm, targets),
        (nodes_hbm, nodes), (gain_hbm, gain), (w_down, wd), (w_gate, wg), (w_up, wu),
    )
    loads = [pltpu.make_async_copy(x, y, load_sem.at[i]) for i, (x, y) in enumerate(pairs)]
    for load in loads:
        load.start()

    loads[0].wait()
    code_row = codes[...].astype(F32)
    code_col = jnp.transpose(jnp.broadcast_to(code_row, (128, NODES)))[:, :1]
    first = lax.broadcasted_iota(jnp.int32, (NODES, NODES), 0)
    second = lax.broadcasted_iota(jnp.int32, (NODES, NODES), 1)
    same = code_col == code_row
    rank_row = jnp.sum(jnp.where(same & (first < second), 1.0, 0.0), axis=0, keepdims=True)
    slot_row = (code_row * CAP + rank_row).astype(jnp.int32)
    place_t[...] = jnp.where(
        lax.broadcasted_iota(jnp.int32, (ROWS, NODES), 0) == slot_row, 1.0, 0.0
    ).astype(BF16)

    def bucket(rows, out):
        out[...] = dot(place_t[...], rows[...]).astype(BF16).reshape(EXPERTS, CAP, D)

    loads[1].wait()
    bucket(d_out, send_g)
    loads[4].wait()
    pl.semaphore_wait(barrier, EXPERTS + 1)

    def rim_copies(low, high, landing, base):
        return [
            pltpu.make_async_remote_copy(
                low, landing.at[pl.ds(0, RIM)], rim_send.at[base], rim_recv.at[base],
                device_id=(before, rep), device_id_type=MESH,
            ),
            pltpu.make_async_remote_copy(
                high, landing.at[pl.ds(RIM, RIM)], rim_send.at[base + 1], rim_recv.at[base + 1],
                device_id=(following, rep), device_id_type=MESH,
            ),
        ]

    rim_first = rim_copies(nodes.at[pl.ds(0, RIM)], nodes.at[pl.ds(NODES - RIM, RIM)], rim_in, 0)
    for copy in rim_first:
        copy.start()

    def exchange(source, landing, slot, core):
        def send(t, sem):
            pltpu.make_async_remote_copy(
                source.at[t], landing.at[me], sem, a2a_recv.at[slot],
                device_id=(t, rep), device_id_type=MESH,
            ).start()

        for a, b in ORDER:
            chip = lax.rem(my + a, 4) * 4 + lax.rem(mx + b, 4)
            send(chip * 2 + core, a2a_send.at[slot, core])

        @pl.when(mc != core)
        def _():
            send(my * 8 + mx * 2 + core, a2a_send.at[slot, 2])

    def exchange_wait(landing, slot):
        part = landing.at[pl.ds(0, EXPERTS - 1)]
        pltpu.make_async_copy(part, part, a2a_recv.at[slot]).wait()

    def exchange_sent(source, slot, core):
        part = source.at[pl.ds(0, CHIPS)]
        pltpu.make_async_copy(part, part, a2a_send.at[slot, core]).wait()

    exchange(send_g, recv_g, 0, 0)
    recv_g[me] = send_g[me]

    loads[2].wait()
    loads[3].wait()
    src = sources[...]
    src = jnp.where(src >= RIM, src - RIM, src + (EXTENT - RIM))
    source_hot = jnp.where(
        lax.broadcasted_iota(jnp.int32, (EXTENT, EDGES), 0) == src, 1.0, 0.0
    ).astype(BF16)
    target_hot = jnp.where(
        lax.broadcasted_iota(jnp.int32, (NODES, EDGES), 0) == targets[...], 1.0, 0.0
    ).astype(BF16)
    count = dot_last(target_hot, source_hot)
    counts[...] = count.astype(BF16)
    inv_s[...] = 1.0 / jnp.maximum(jnp.sum(count, axis=1, keepdims=True), 1.0)
    total[...] = dot(counts[:, pl.ds(0, NODES)], nodes[...])
    loads[5].wait()
    for copy in rim_first:
        copy.wait_recv()
    total[...] += dot(counts[:, pl.ds(NODES, 2 * RIM)], rim_in[...])
    gain_row = gain[...].reshape(1, D)

    def normalize(i, carry):
        at = chunk(i, 32)
        mixed = nodes[at, :].astype(F32) + total[at, :] * inv_s[at, :]
        scaling = lax.rsqrt(jnp.mean(mixed * mixed, axis=1, keepdims=True) + 1e-05)
        scale_s[at, :] = scaling
        norm = mixed * scaling
        normal[at, :] = norm
        dmean[at, :] = (norm * gain_row).astype(BF16)
        return carry

    lax.fori_loop(0, NODES // 32, normalize, 0)
    bucket(dmean, send_r)
    exchange(send_r, recv_r, 1, 0)
    recv_r[me] = send_r[me]

    def turn(source, out):
        def body(i, carry):
            out[chunk(i, 128), :] = jnp.transpose(source[:, chunk(i, 128)])
            return carry

        lax.fori_loop(0, FF // 128, body, 0)

    loads[6].wait()
    turn(wd, wdt)
    for slot, source in enumerate((send_g, send_r)):
        exchange_sent(source, slot, 0)
    exchange(send_g, recv_g, 0, 1)
    exchange(send_r, recv_r, 1, 1)
    loads[7].wait()
    turn(wg, wgt)
    loads[8].wait()
    turn(wu, wut)

    def flat(ref):
        return ref[...].reshape(ROWS, D)

    def mod(i):
        return lax.rem(i + 2 * REPS, REPS)

    def parts(i):
        low = mod(rep - 1 - i) * SLICE
        high = mod(rep + 1 + i) * SLICE + PART
        return [pl.ds(pl.multiple_of(x, PART), PART) for x in (low, high)]

    def item_rows(i, ref):
        low, high = parts(i)
        return jnp.concatenate([ref[low, :], ref[high, :]], axis=0)

    def hop(d, k, j):
        source = partial.at[0, j, d] if k == 0 else ring.at[k - 1, j, d]
        return pltpu.make_async_remote_copy(
            source, ring.at[k, j, d], ring_send.at[k, j, d], ring_recv.at[k, j, d],
            device_id=(me, rep_up if d == 0 else rep_down), device_id_type=MESH,
        )

    def item_back(i):
        bh_s[...] = dot_last(item_rows(i, wdt), flat(recv_g))

    def item(i, back=True):
        gate_s[...] = dot_last(item_rows(i, wgt), flat(recv_r))
        up_s[...] = dot_last(item_rows(i, wut), flat(recv_r))
        if back:
            item_back(i)
        for d, units in enumerate(parts(i)):

            def act(n, carry):
                rows = pl.ds(pl.multiple_of(d * PART + n * 16, 16), 16)
                here = pl.ds(pl.multiple_of(units.start + n * 16, 16), 16)
                g, u, b = gate_s[rows, :], up_s[rows, :], bh_s[rows, :]
                s = jax.nn.sigmoid(g)
                silu = g * s
                hid_t[here, :] = (silu * u).astype(BF16)
                dgate_t[here, :] = (b * u * s * (1.0 + g * (1.0 - s))).astype(BF16)
                dup_t[here, :] = (b * silu).astype(BF16)
                return carry

            lax.fori_loop(0, PART // 16, act, 0)
        for j, (left, right) in enumerate(((hid_t, recv_g), (dgate_t, recv_r), (dup_t, recv_r))):
            g = dot(item_rows(i, left), flat(right)).astype(BF16)
            for d in range(2):
                partial[i, j, d] = g[d * PART : (d + 1) * PART, :]
            if i == 0:
                for d in range(2):
                    hop(d, 0, j).start()

    def serve(k, j):
        for d in range(2):
            hop(d, k - 1, j).wait_recv()

            def add(i, carry):
                at = chunk(i, 16)
                ring[k - 1, j, d, at, :] = (
                    ring[k - 1, j, d, at, :].astype(F32) + partial[k, j, d, at, :].astype(F32)
                ).astype(BF16)
                return carry

            lax.fori_loop(0, PART // 16, add, 0)
            hop(d, k, j).start()

    exchange_wait(recv_g, 0)
    item_back(0)
    exchange_wait(recv_r, 1)
    item(0, back=False)
    item(1)
    item(2)
    serve(1, 0)
    serve(1, 1)
    item(3)
    serve(1, 2)
    item(4)
    serve(2, 0)
    item(5)
    serve(2, 1)
    item(6)
    serve(2, 2)
    item(7)
    serve(3, 0)

    def project(terms, out):
        def body(b, carry):
            at = chunk(b, 256)
            y = dot(terms[0][0][at, :], terms[0][1][...])
            for w, x in terms[1:]:
                y = y + dot(w[at, :], x[...])
            out[:, :, at] = jnp.transpose(y).astype(BF16).reshape(EXPERTS, CAP, 256)
            return carry

        lax.fori_loop(0, D // 256, body, 0)

    project(((wd, hid_t),), back_e)
    for core in range(2):
        exchange(back_e, ret_e, 2, core)
    ret_e[me] = back_e[me]
    serve(3, 1)
    project(((wg, dgate_t), (wu, dup_t)), back_d)
    for core in range(2):
        exchange(back_d, ret_d, 3, core)
    ret_d[me] = back_d[me]
    serve(3, 2)
    serve(4, 0)
    rank_col = jnp.sum(jnp.where(same & (second < first), 1.0, 0.0), axis=1, keepdims=True)
    slot_col = (code_col * CAP + rank_col).astype(jnp.int32)
    place[...] = jnp.where(
        lax.broadcasted_iota(jnp.int32, (NODES, ROWS), 1) == slot_col, 1.0, 0.0
    ).astype(BF16)
    counts_t[...] = jnp.transpose(counts[...].astype(F32)).astype(BF16)
    serve(4, 1)
    serve(4, 2)
    for j in range(3):
        serve(5, j)

    exchange_wait(ret_e, 2)
    total[...] = dot(place[...], flat(ret_e))

    def forward_out(i, carry):
        at = chunk(i, 32)
        layer_out[at, :] = (nodes[at, :].astype(F32) + total[at, :]).astype(BF16)
        return carry

    lax.fori_loop(0, NODES // 32, forward_out, 0)
    exchange_wait(ret_d, 3)
    total[...] = dot(place[...], flat(ret_d))

    def norm_back(i, carry):
        at = chunk(i, 32)
        d_norm = total[at, :] * gain_row
        norm = normal[at, :]
        d_mixed = scale_s[at, :] * (d_norm - norm * jnp.mean(d_norm * norm, axis=1, keepdims=True))
        dmean[at, :] = (d_mixed * inv_s[at, :]).astype(BF16)
        total[at, :] = d_out[at, :].astype(F32) + d_mixed
        return carry

    lax.fori_loop(0, NODES // 32, norm_back, 0)
    rim_out[...] = dot(counts_t[pl.ds(NODES, 2 * RIM), :], dmean[...]).astype(BF16)
    rim_last = rim_copies(rim_out.at[pl.ds(RIM, RIM)], rim_out.at[pl.ds(0, RIM)], rim_back, 2)
    for copy in rim_last:
        copy.start()
    serve(6, 0)
    total[...] += dot(counts_t[pl.ds(0, NODES), :], dmean[...])
    serve(6, 1)
    serve(6, 2)
    for copy in rim_last:
        copy.wait_recv()
    total[pl.ds(0, RIM), :] += rim_back[pl.ds(RIM, RIM), :].astype(F32)
    total[pl.ds(NODES - RIM, RIM), :] += rim_back[pl.ds(0, RIM), :].astype(F32)

    def node_out(i, carry):
        at = chunk(i, 32)
        d_nodes[at, :] = total[at, :].astype(BF16)
        return carry

    lax.fori_loop(0, NODES // 32, node_out, 0)
    for copy in rim_first + rim_last:
        copy.wait_send()
    for slot, source in enumerate((send_g, send_r, back_e, back_d)):
        for core in range(2):
            if slot > 1 or core == 1:
                exchange_sent(source, slot, core)
        part = source.at[0]
        pltpu.make_async_copy(part, part, a2a_send.at[slot, 2]).wait()
    for k in range(REPS - 2):
        for j in range(3):
            for d in range(2):
                hop(d, k, j).wait_send()

    for j, out in enumerate((grad_down, grad_gate, grad_up)):
        for d in range(2):
            hop(d, 6, j).wait_recv()

            def last(i, carry):
                at = chunk(i, 16)
                out[pl.ds(pl.multiple_of(d * PART + i * 16, 16), 16), :] = (
                    ring[6, j, d, at, :].astype(F32) + partial[7, j, d, at, :].astype(F32)
                )
                return carry

            lax.fori_loop(0, PART // 16, last, 0)
    for j in range(3):
        for d in range(2):
            hop(d, 6, j).wait_send()


def on_device(node_feats, edge_src, edge_dst, node_codes, norm_gain, w_gate, w_up, w_down_t, d_out):
    hbm = pl.BlockSpec(memory_space=pl.ANY)
    vmem = pltpu.VMEM
    sem = pltpu.SemaphoreType.DMA
    weight = vmem((D, FF), BF16)
    weight_t = vmem((FF, D), BF16)
    buckets = vmem((EXPERTS, CAP, D), BF16)
    act_t = vmem((FF, ROWS), BF16)
    rows = vmem((NODES, D), BF16)
    wide = vmem((NODES, D), F32)
    item = vmem((SLICE, ROWS), F32)
    rims = vmem((2 * RIM, D), BF16)
    outs = [jax.ShapeDtypeStruct((NODES, D), BF16)] * 2 + [
        jax.ShapeDtypeStruct((SLICE, D), F32)
    ] * 3
    out = pl.pallas_call(
        kernel,
        out_shape=[vmem(x.shape, x.dtype) for x in outs],
        in_specs=[hbm] * 9,
        out_specs=[pl.BlockSpec(memory_space=vmem)] * 5,
        scratch_shapes=[
            rows,
            vmem((1, EDGES), jnp.int32),
            vmem((1, EDGES), jnp.int32),
            vmem((1, NODES), jnp.int32),
            vmem((D,), F32),
            rows,
        ]
        + [weight] * 3
        + [weight_t] * 3
        + [vmem((REPS, 3, 2, PART, D), BF16), vmem((REPS - 1, 3, 2, PART, D), BF16)]
        + [buckets] * 8
        + [act_t] * 3
        + [item] * 3
        + [
            wide,
            wide,
            vmem((NODES, EXTENT), BF16),
            vmem((EXTENT, NODES), BF16),
            vmem((NODES, ROWS), BF16),
            vmem((ROWS, NODES), BF16),
            vmem((NODES, 1), F32),
            vmem((NODES, 1), F32),
        ]
        + [rims] * 3
        + [
            rows,
            sem((9,)),
            sem((4,)),
            sem((4,)),
            sem((4, 3)),
            sem((4,)),
            sem((REPS - 1, 3, 2)),
            sem((REPS - 1, 3, 2)),
        ],
        compiler_params=pltpu.CompilerParams(
            collective_id=0, has_side_effects=True, vmem_limit_bytes=58 * 2**20
        ),
        name="graph_moe",
    )(
        node_feats[0], edge_src, edge_dst, node_codes.reshape(1, NODES), norm_gain,
        w_gate[0], w_up[0], w_down_t[0], d_out[0],
    )
    layer_out, d_nodes, *grads = out
    return (layer_out[None], d_nodes[None], *(g.T[None] for g in grads))


def solution(mesh):
    rows = P("rep", "expert", None)
    edges = P("rep", "expert")
    weights = P("expert", None, None)
    grads = P("expert", None, "rep")
    return jax.shard_map(
        on_device,
        mesh=mesh,
        in_specs=(rows, edges, edges, rows, P(), weights, weights, weights, rows),
        out_specs=(rows, rows, grads, grads, grads),
        check_vma=False,
    )
```

```python
import jax
import jax.numpy as jnp
from jax import lax
from jax.experimental import pallas as pl
from jax.experimental.pallas import tpu as pltpu
from jax.sharding import PartitionSpec as P

MESH = pl.DeviceIdType.MESH
F32 = jnp.float32
BF16 = jnp.bfloat16

D = 768
FF = 1536
NODES = 256
RIM = 64
EXTENT = NODES + 2 * RIM
EDGES = 1024
EXPERTS = 32
CAP = 16
ROWS = EXPERTS * CAP
REPS = 8
SLICE = FF // REPS
PART = SLICE // 2


def partner_order():
    hops = (0, 1, 2, 1)
    offsets = [(a, b) for a in range(4) for b in range(4)][1:]
    offsets.sort(key=lambda o: -(hops[o[0]] + hops[o[1]]))
    order = []
    for a, b in offsets:
        for p in ((a, b), ((4 - a) % 4, (4 - b) % 4)):
            if p not in order:
                order.append(p)
    return order


ORDER = partner_order()
CHIPS = len(ORDER)


def dot(a, b):
    return jnp.dot(a, b, preferred_element_type=F32)


def dot_last(a, b):
    return lax.dot_general(a, b, (((1,), (1,)), ((), ())), preferred_element_type=F32)


def chunk(i, size):
    return pl.ds(pl.multiple_of(i * size, size), size)


def kernel(
    nodes_hbm, sources_hbm, targets_hbm, codes_hbm, gain_hbm, w_gate, w_up, w_down, d_out_hbm,
    layer_out, d_nodes, grad_gate, grad_up, grad_down,
    nodes, sources, targets, codes, gain, d_out,
    wg, wu, wd, wgt, wut, wdt, partial, ring,
    send_g, send_r, recv_g, recv_r, back_e, back_d, ret_e, ret_d,
    hid_t, dgate_t, dup_t, bh_s, gate_s, up_s,
    normal, total, counts, counts_t, place, place_t, scale_s, inv_s,
    rim_in, rim_out, rim_back, dmean,
    load_sem, rim_send, rim_recv, a2a_send, a2a_recv, ring_send, ring_recv,
):
    me = lax.axis_index("expert")
    rep = lax.axis_index("rep")
    my, mx, mc = me // 8, lax.rem(me // 2, 4), lax.rem(me, 2)
    following, before = lax.rem(me + 1, EXPERTS), lax.rem(me + EXPERTS - 1, EXPERTS)
    rep_up, rep_down = lax.rem(rep + 1, REPS), lax.rem(rep + REPS - 1, REPS)

    pairs = (
        (codes_hbm, codes), (d_out_hbm, d_out), (sources_hbm, sources), (targets_hbm, targets),
        (nodes_hbm, nodes), (gain_hbm, gain), (w_down, wd), (w_gate, wg), (w_up, wu),
    )
    loads = [pltpu.make_async_copy(x, y, load_sem.at[i]) for i, (x, y) in enumerate(pairs)]
    for n in (0, 1, 4):
        loads[n].start()

    barrier = pltpu.get_barrier_semaphore()

    def greet(i, carry):
        pl.semaphore_signal(
            barrier, inc=1, device_id=(lax.rem(me + i, EXPERTS), rep), device_id_type=MESH
        )
        return carry

    lax.fori_loop(1, EXPERTS, greet, 0)
    for z in (rep_up, rep_down):
        pl.semaphore_signal(barrier, inc=1, device_id=(me, z), device_id_type=MESH)
    for n in (2, 3, 5, 6, 7, 8):
        loads[n].start()

    loads[0].wait()
    code_row = codes[...].astype(F32)
    code_col = jnp.transpose(jnp.broadcast_to(code_row, (128, NODES)))[:, :1]
    first = lax.broadcasted_iota(jnp.int32, (NODES, NODES), 0)
    second = lax.broadcasted_iota(jnp.int32, (NODES, NODES), 1)
    same = code_col == code_row
    rank_row = jnp.sum(jnp.where(same & (first < second), 1.0, 0.0), axis=0, keepdims=True)
    slot_row = (code_row * CAP + rank_row).astype(jnp.int32)
    place_t[...] = jnp.where(
        lax.broadcasted_iota(jnp.int32, (ROWS, NODES), 0) == slot_row, 1.0, 0.0
    ).astype(BF16)

    def bucket(rows, out):
        out[...] = dot(place_t[...], rows[...]).astype(BF16).reshape(EXPERTS, CAP, D)

    loads[1].wait()
    bucket(d_out, send_g)
    loads[4].wait()
    pl.semaphore_wait(barrier, EXPERTS + 1)

    def rim_copies(low, high, landing, base):
        return [
            pltpu.make_async_remote_copy(
                low, landing.at[pl.ds(0, RIM)], rim_send.at[base], rim_recv.at[base],
                device_id=(before, rep), device_id_type=MESH,
            ),
            pltpu.make_async_remote_copy(
                high, landing.at[pl.ds(RIM, RIM)], rim_send.at[base + 1], rim_recv.at[base + 1],
                device_id=(following, rep), device_id_type=MESH,
            ),
        ]

    rim_first = rim_copies(nodes.at[pl.ds(0, RIM)], nodes.at[pl.ds(NODES - RIM, RIM)], rim_in, 0)
    for copy in rim_first:
        copy.start()

    def exchange(source, landing, slot, core):
        def send(t, sem):
            pltpu.make_async_remote_copy(
                source.at[t], landing.at[me], sem, a2a_recv.at[slot],
                device_id=(t, rep), device_id_type=MESH,
            ).start()

        for a, b in ORDER:
            chip = lax.rem(my + a, 4) * 4 + lax.rem(mx + b, 4)
            send(chip * 2 + core, a2a_send.at[slot, core])

        @pl.when(mc != core)
        def _():
            send(my * 8 + mx * 2 + core, a2a_send.at[slot, 2])

    def exchange_wait(landing, slot):
        part = landing.at[pl.ds(0, EXPERTS - 1)]
        pltpu.make_async_copy(part, part, a2a_recv.at[slot]).wait()

    def exchange_sent(source, slot, core):
        part = source.at[pl.ds(0, CHIPS)]
        pltpu.make_async_copy(part, part, a2a_send.at[slot, core]).wait()

    exchange(send_g, recv_g, 0, 0)
    recv_g[me] = send_g[me]

    loads[2].wait()
    loads[3].wait()
    src = sources[...]
    src = jnp.where(src >= RIM, src - RIM, src + (EXTENT - RIM))
    source_hot = jnp.where(
        lax.broadcasted_iota(jnp.int32, (EXTENT, EDGES), 0) == src, 1.0, 0.0
    ).astype(BF16)
    target_hot = jnp.where(
        lax.broadcasted_iota(jnp.int32, (NODES, EDGES), 0) == targets[...], 1.0, 0.0
    ).astype(BF16)
    count = dot_last(target_hot, source_hot)
    counts[...] = count.astype(BF16)
    inv_s[...] = 1.0 / jnp.maximum(jnp.sum(count, axis=1, keepdims=True), 1.0)
    total[...] = dot(counts[:, pl.ds(0, NODES)], nodes[...])
    loads[5].wait()
    for copy in rim_first:
        copy.wait_recv()
    total[...] += dot(counts[:, pl.ds(NODES, 2 * RIM)], rim_in[...])
    gain_row = gain[...].reshape(1, D)

    def normalize(i, carry):
        at = chunk(i, 32)
        mixed = nodes[at, :].astype(F32) + total[at, :] * inv_s[at, :]
        scaling = lax.rsqrt(jnp.mean(mixed * mixed, axis=1, keepdims=True) + 1e-05)
        scale_s[at, :] = scaling
        norm = mixed * scaling
        normal[at, :] = norm
        dmean[at, :] = (norm * gain_row).astype(BF16)
        return carry

    lax.fori_loop(0, NODES // 32, normalize, 0, unroll=8)
    bucket(dmean, send_r)
    exchange(send_r, recv_r, 1, 0)
    recv_r[me] = send_r[me]

    def turn(source, out):
        def body(i, carry):
            out[chunk(i, 128), :] = jnp.transpose(source[:, chunk(i, 128)])
            return carry

        lax.fori_loop(0, FF // 128, body, 0)

    loads[6].wait()
    turn(wd, wdt)
    for slot, source in enumerate((send_g, send_r)):
        exchange_sent(source, slot, 0)
    exchange(send_g, recv_g, 0, 1)
    exchange(send_r, recv_r, 1, 1)
    loads[7].wait()
    turn(wg, wgt)
    loads[8].wait()
    turn(wu, wut)

    def flat(ref):
        return ref[...].reshape(ROWS, D)

    def mod(i):
        return lax.rem(i + 2 * REPS, REPS)

    def parts(i):
        low = mod(rep - 1 - i) * SLICE
        high = mod(rep + 1 + i) * SLICE + PART
        return [pl.ds(pl.multiple_of(x, PART), PART) for x in (low, high)]

    def item_rows(i, ref):
        low, high = parts(i)
        return jnp.concatenate([ref[low, :], ref[high, :]], axis=0)

    def hop(d, k, j):
        source = partial.at[0, j, d] if k == 0 else ring.at[k - 1, j, d]
        return pltpu.make_async_remote_copy(
            source, ring.at[k, j, d], ring_send.at[k, j, d], ring_recv.at[k, j, d],
            device_id=(me, rep_up if d == 0 else rep_down), device_id_type=MESH,
        )

    def item_back(i):
        bh_s[...] = dot_last(item_rows(i, wdt), flat(recv_g))

    def item(i, back=True):
        gate_s[...] = dot_last(item_rows(i, wgt), flat(recv_r))
        up_s[...] = dot_last(item_rows(i, wut), flat(recv_r))
        if back:
            item_back(i)
        for d, units in enumerate(parts(i)):

            def act(n, carry):
                rows = pl.ds(pl.multiple_of(d * PART + n * 16, 16), 16)
                here = pl.ds(pl.multiple_of(units.start + n * 16, 16), 16)
                g, u, b = gate_s[rows, :], up_s[rows, :], bh_s[rows, :]
                s = jax.nn.sigmoid(g)
                silu = g * s
                hid_t[here, :] = (silu * u).astype(BF16)
                dgate_t[here, :] = (b * u * s * (1.0 + g * (1.0 - s))).astype(BF16)
                dup_t[here, :] = (b * silu).astype(BF16)
                return carry

            lax.fori_loop(0, PART // 16, act, 0, unroll=6 if i == 0 else 2)
        for j, (left, right) in enumerate(((hid_t, recv_g), (dgate_t, recv_r), (dup_t, recv_r))):
            g = dot(item_rows(i, left), flat(right)).astype(BF16)
            for d in range(2):
                partial[i, j, d] = g[d * PART : (d + 1) * PART, :]
            if i == 0:
                for d in range(2):
                    hop(d, 0, j).start()

    def serve(k, j):
        for d in range(2):
            hop(d, k - 1, j).wait_recv()

            def add(i, carry):
                at = chunk(i, 16)
                ring[k - 1, j, d, at, :] = (
                    ring[k - 1, j, d, at, :].astype(F32) + partial[k, j, d, at, :].astype(F32)
                ).astype(BF16)
                return carry

            lax.fori_loop(0, PART // 16, add, 0, unroll=3)
            hop(d, k, j).start()

    exchange_wait(recv_g, 0)
    item_back(0)
    exchange_wait(recv_r, 1)
    item(0, back=False)
    item(1)
    item(2)
    serve(1, 0)
    serve(1, 1)
    item(3)
    serve(1, 2)
    item(4)
    serve(2, 0)
    item(5)
    serve(2, 1)
    item(6)
    serve(2, 2)
    item(7)
    serve(3, 0)

    def project(terms, out):
        def body(b, carry):
            at = chunk(b, 256)
            y = dot(terms[0][0][at, :], terms[0][1][...])
            for w, x in terms[1:]:
                y = y + dot(w[at, :], x[...])
            out[:, :, at] = jnp.transpose(y).astype(BF16).reshape(EXPERTS, CAP, 256)
            return carry

        lax.fori_loop(0, D // 256, body, 0)

    project(((wd, hid_t),), back_e)
    for core in range(2):
        exchange(back_e, ret_e, 2, core)
    ret_e[me] = back_e[me]
    serve(3, 1)
    project(((wg, dgate_t), (wu, dup_t)), back_d)
    for core in range(2):
        exchange(back_d, ret_d, 3, core)
    ret_d[me] = back_d[me]
    serve(3, 2)
    serve(4, 0)
    rank_col = jnp.sum(jnp.where(same & (second < first), 1.0, 0.0), axis=1, keepdims=True)
    slot_col = (code_col * CAP + rank_col).astype(jnp.int32)
    place[...] = jnp.where(
        lax.broadcasted_iota(jnp.int32, (NODES, ROWS), 1) == slot_col, 1.0, 0.0
    ).astype(BF16)
    counts_t[...] = jnp.transpose(counts[...].astype(F32)).astype(BF16)
    serve(4, 1)
    serve(4, 2)
    for j in range(3):
        serve(5, j)

    exchange_wait(ret_e, 2)
    total[...] = dot(place[...], flat(ret_e))

    def forward_out(i, carry):
        at = chunk(i, 32)
        layer_out[at, :] = (nodes[at, :].astype(F32) + total[at, :]).astype(BF16)
        return carry

    lax.fori_loop(0, NODES // 32, forward_out, 0)
    exchange_wait(ret_d, 3)
    total[...] = dot(place[...], flat(ret_d))

    def norm_back(i, carry):
        at = chunk(i, 32)
        d_norm = total[at, :] * gain_row
        norm = normal[at, :]
        d_mixed = scale_s[at, :] * (d_norm - norm * jnp.mean(d_norm * norm, axis=1, keepdims=True))
        dmean[at, :] = (d_mixed * inv_s[at, :]).astype(BF16)
        total[at, :] = d_out[at, :].astype(F32) + d_mixed
        return carry

    lax.fori_loop(0, NODES // 32, norm_back, 0, unroll=4)
    rim_out[...] = dot(counts_t[pl.ds(NODES, 2 * RIM), :], dmean[...]).astype(BF16)
    rim_last = rim_copies(rim_out.at[pl.ds(RIM, RIM)], rim_out.at[pl.ds(0, RIM)], rim_back, 2)
    for copy in rim_last:
        copy.start()
    serve(6, 0)
    total[...] += dot(counts_t[pl.ds(0, NODES), :], dmean[...])
    serve(6, 1)
    serve(6, 2)
    for copy in rim_last:
        copy.wait_recv()
    total[pl.ds(0, RIM), :] += rim_back[pl.ds(RIM, RIM), :].astype(F32)
    total[pl.ds(NODES - RIM, RIM), :] += rim_back[pl.ds(0, RIM), :].astype(F32)

    def node_out(i, carry):
        at = chunk(i, 32)
        d_nodes[at, :] = total[at, :].astype(BF16)
        return carry

    lax.fori_loop(0, NODES // 32, node_out, 0)
    for copy in rim_first + rim_last:
        copy.wait_send()
    for slot, source in enumerate((send_g, send_r, back_e, back_d)):
        for core in range(2):
            if slot > 1 or core == 1:
                exchange_sent(source, slot, core)
        part = source.at[0]
        pltpu.make_async_copy(part, part, a2a_send.at[slot, 2]).wait()
    for k in range(REPS - 2):
        for j in range(3):
            for d in range(2):
                hop(d, k, j).wait_send()

    for j, out in enumerate((grad_down, grad_gate, grad_up)):
        for d in range(2):
            hop(d, 6, j).wait_recv()

            def last(i, carry):
                at = chunk(i, 16)
                out[pl.ds(pl.multiple_of(d * PART + i * 16, 16), 16), :] = (
                    ring[6, j, d, at, :].astype(F32) + partial[7, j, d, at, :].astype(F32)
                )
                return carry

            lax.fori_loop(0, PART // 16, last, 0, unroll=6)
    for j in range(3):
        for d in range(2):
            hop(d, 6, j).wait_send()


def finish(*refs):
    count = (len(refs) - 1) // 2
    copies = [
        pltpu.make_async_copy(refs[i], refs[count + i], refs[-1].at[i]) for i in range(count)
    ]
    for copy in copies:
        copy.start()
    for copy in copies:
        copy.wait()


def on_device(node_feats, edge_src, edge_dst, node_codes, norm_gain, w_gate, w_up, w_down_t, d_out):
    hbm = pl.BlockSpec(memory_space=pl.ANY)
    vmem = pltpu.VMEM
    sem = pltpu.SemaphoreType.DMA
    weight = vmem((D, FF), BF16)
    weight_t = vmem((FF, D), BF16)
    buckets = vmem((EXPERTS, CAP, D), BF16)
    act_t = vmem((FF, ROWS), BF16)
    rows = vmem((NODES, D), BF16)
    wide = vmem((NODES, D), F32)
    item = vmem((SLICE, ROWS), F32)
    rims = vmem((2 * RIM, D), BF16)
    outs = [jax.ShapeDtypeStruct((NODES, D), BF16)] * 2 + [
        jax.ShapeDtypeStruct((SLICE, D), F32)
    ] * 3
    out = pl.pallas_call(
        kernel,
        out_shape=[vmem(x.shape, x.dtype) for x in outs],
        in_specs=[hbm] * 9,
        out_specs=[pl.BlockSpec(memory_space=vmem)] * 5,
        scratch_shapes=[
            rows,
            vmem((1, EDGES), jnp.int32),
            vmem((1, EDGES), jnp.int32),
            vmem((1, NODES), jnp.int32),
            vmem((D,), F32),
            rows,
        ]
        + [weight] * 3
        + [weight_t] * 3
        + [vmem((REPS, 3, 2, PART, D), BF16), vmem((REPS - 1, 3, 2, PART, D), BF16)]
        + [buckets] * 8
        + [act_t] * 3
        + [item] * 3
        + [
            wide,
            wide,
            vmem((NODES, EXTENT), BF16),
            vmem((EXTENT, NODES), BF16),
            vmem((NODES, ROWS), BF16),
            vmem((ROWS, NODES), BF16),
            vmem((NODES, 1), F32),
            vmem((NODES, 1), F32),
        ]
        + [rims] * 3
        + [
            rows,
            sem((9,)),
            sem((4,)),
            sem((4,)),
            sem((4, 3)),
            sem((4,)),
            sem((REPS - 1, 3, 2)),
            sem((REPS - 1, 3, 2)),
        ],
        compiler_params=pltpu.CompilerParams(
            collective_id=0, has_side_effects=True, vmem_limit_bytes=58 * 2**20
        ),
        name="graph_moe",
    )(
        node_feats[0], edge_src, edge_dst, node_codes.reshape(1, NODES), norm_gain,
        w_gate[0], w_up[0], w_down_t[0], d_out[0],
    )
    layer_out, d_nodes, *grads = pl.pallas_call(
        finish,
        out_shape=outs,
        in_specs=[pl.BlockSpec(memory_space=vmem)] * 5,
        out_specs=[hbm] * 5,
        scratch_shapes=[sem((5,))],
        name="results",
    )(*(pltpu.with_memory_space_constraint(x, pltpu.VMEM) for x in out))
    return (layer_out[None], d_nodes[None], *(g.T[None] for g in grads))


def solution(mesh):
    rows = P("rep", "expert", None)
    edges = P("rep", "expert")
    weights = P("expert", None, None)
    grads = P("expert", None, "rep")
    return jax.shard_map(
        on_device,
        mesh=mesh,
        in_specs=(rows, edges, edges, rows, P(), weights, weights, weights, rows),
        out_specs=(rows, rows, grads, grads, grads),
        check_vma=False,
    )
```

```python
import jax
import jax.numpy as jnp
from jax import lax
from jax.experimental import pallas as pl
from jax.experimental.pallas import tpu as pltpu
from jax.sharding import PartitionSpec as P

MESH = pl.DeviceIdType.MESH
F32 = jnp.float32
BF16 = jnp.bfloat16

D = 768
FF = 1536
NODES = 256
RIM = 64
EXTENT = NODES + 2 * RIM
EDGES = 1024
EXPERTS = 32
CAP = 16
ROWS = EXPERTS * CAP
REPS = 8
SLICE = FF // REPS
PART = SLICE // 2


def partner_order():
    hops = (0, 1, 2, 1)
    offsets = [(a, b) for a in range(4) for b in range(4)][1:]
    offsets.sort(key=lambda o: -(hops[o[0]] + hops[o[1]]))
    order = []
    for a, b in offsets:
        for p in ((a, b), ((4 - a) % 4, (4 - b) % 4)):
            if p not in order:
                order.append(p)
    return order


ORDER = partner_order()
CHIPS = len(ORDER)


def dot(a, b):
    return jnp.dot(a, b, preferred_element_type=F32)


def dot_last(a, b):
    return lax.dot_general(a, b, (((1,), (1,)), ((), ())), preferred_element_type=F32)


def chunk(i, size):
    return pl.ds(pl.multiple_of(i * size, size), size)


def kernel(
    nodes_hbm, sources_hbm, targets_hbm, codes_hbm, gain_hbm, w_gate, w_up, w_down, d_out_hbm,
    layer_out, d_nodes, grad_gate, grad_up, grad_down,
    nodes, sources, targets, codes, gain, d_out,
    wg, wu, wd, wgt, wut, wdt, partial, ring,
    send_g, send_r, recv_g, recv_r, back_e, back_d, ret_e, ret_d,
    hid_t, dgate_t, dup_t, bh_s, gate_s, up_s,
    normal, total, counts, counts_t, place, place_t, scale_s, inv_s,
    rim_in, rim_out, rim_back, dmean,
    load_sem, rim_send, rim_recv, a2a_send, a2a_recv, ring_send, ring_recv,
):
    me = lax.axis_index("expert")
    rep = lax.axis_index("rep")
    my, mx, mc = me // 8, lax.rem(me // 2, 4), lax.rem(me, 2)
    following, before = lax.rem(me + 1, EXPERTS), lax.rem(me + EXPERTS - 1, EXPERTS)
    rep_up, rep_down = lax.rem(rep + 1, REPS), lax.rem(rep + REPS - 1, REPS)

    pairs = (
        (codes_hbm, codes), (d_out_hbm, d_out), (sources_hbm, sources), (targets_hbm, targets),
        (nodes_hbm, nodes), (gain_hbm, gain), (w_down, wd), (w_gate, wg), (w_up, wu),
    )
    loads = [pltpu.make_async_copy(x, y, load_sem.at[i]) for i, (x, y) in enumerate(pairs)]
    for n in (0, 1, 4):
        loads[n].start()

    barrier = pltpu.get_barrier_semaphore()

    def greet(i, carry):
        pl.semaphore_signal(
            barrier, inc=1, device_id=(lax.rem(me + i, EXPERTS), rep), device_id_type=MESH
        )
        return carry

    lax.fori_loop(1, EXPERTS, greet, 0)
    for z in (rep_up, rep_down):
        pl.semaphore_signal(barrier, inc=1, device_id=(me, z), device_id_type=MESH)
    for n in (2, 3, 5, 6, 7, 8):
        loads[n].start()

    loads[0].wait()
    code_row = codes[...].astype(F32)
    code_col = jnp.transpose(jnp.broadcast_to(code_row, (128, NODES)))[:, :1]
    first = lax.broadcasted_iota(jnp.int32, (NODES, NODES), 0)
    second = lax.broadcasted_iota(jnp.int32, (NODES, NODES), 1)
    same = code_col == code_row
    rank_row = jnp.sum(jnp.where(same & (first < second), 1.0, 0.0), axis=0, keepdims=True)
    slot_row = (code_row * CAP + rank_row).astype(jnp.int32)
    place_t[...] = jnp.where(
        lax.broadcasted_iota(jnp.int32, (ROWS, NODES), 0) == slot_row, 1.0, 0.0
    ).astype(BF16)

    def bucket(rows, out):
        out[...] = dot(place_t[...], rows[...]).astype(BF16).reshape(EXPERTS, CAP, D)

    loads[1].wait()
    bucket(d_out, send_g)
    loads[4].wait()
    pl.semaphore_wait(barrier, EXPERTS + 1)

    def rim_copies(low, high, landing, base):
        return [
            pltpu.make_async_remote_copy(
                low, landing.at[pl.ds(0, RIM)], rim_send.at[base], rim_recv.at[base],
                device_id=(before, rep), device_id_type=MESH,
            ),
            pltpu.make_async_remote_copy(
                high, landing.at[pl.ds(RIM, RIM)], rim_send.at[base + 1], rim_recv.at[base + 1],
                device_id=(following, rep), device_id_type=MESH,
            ),
        ]

    rim_first = rim_copies(nodes.at[pl.ds(0, RIM)], nodes.at[pl.ds(NODES - RIM, RIM)], rim_in, 0)
    for copy in rim_first:
        copy.start()

    def exchange(source, landing, slot, core):
        def send(t, sem):
            pltpu.make_async_remote_copy(
                source.at[t], landing.at[me], sem, a2a_recv.at[slot],
                device_id=(t, rep), device_id_type=MESH,
            ).start()

        for a, b in ORDER:
            chip = lax.rem(my + a, 4) * 4 + lax.rem(mx + b, 4)
            send(chip * 2 + core, a2a_send.at[slot, core])

        @pl.when(mc != core)
        def _():
            send(my * 8 + mx * 2 + core, a2a_send.at[slot, 2])

    def exchange_wait(landing, slot):
        part = landing.at[pl.ds(0, EXPERTS - 1)]
        pltpu.make_async_copy(part, part, a2a_recv.at[slot]).wait()

    def exchange_sent(source, slot, core):
        part = source.at[pl.ds(0, CHIPS)]
        pltpu.make_async_copy(part, part, a2a_send.at[slot, core]).wait()

    exchange(send_g, recv_g, 0, 0)
    recv_g[me] = send_g[me]

    loads[2].wait()
    loads[3].wait()
    src = sources[...]
    src = jnp.where(src >= RIM, src - RIM, src + (EXTENT - RIM))
    source_hot = jnp.where(
        lax.broadcasted_iota(jnp.int32, (EXTENT, EDGES), 0) == src, 1.0, 0.0
    ).astype(BF16)
    target_hot = jnp.where(
        lax.broadcasted_iota(jnp.int32, (NODES, EDGES), 0) == targets[...], 1.0, 0.0
    ).astype(BF16)
    count = dot_last(target_hot, source_hot)
    counts[...] = count.astype(BF16)
    inv_s[...] = 1.0 / jnp.maximum(jnp.sum(count, axis=1, keepdims=True), 1.0)
    total[...] = dot(counts[:, pl.ds(0, NODES)], nodes[...])
    loads[5].wait()
    for copy in rim_first:
        copy.wait_recv()
    total[...] += dot(counts[:, pl.ds(NODES, 2 * RIM)], rim_in[...])
    gain_row = gain[...].reshape(1, D)

    def normalize(i, carry):
        at = chunk(i, 32)
        mixed = nodes[at, :].astype(F32) + total[at, :] * inv_s[at, :]
        scaling = lax.rsqrt(jnp.mean(mixed * mixed, axis=1, keepdims=True) + 1e-05)
        scale_s[at, :] = scaling
        norm = mixed * scaling
        normal[at, :] = norm
        dmean[at, :] = (norm * gain_row).astype(BF16)
        return carry

    lax.fori_loop(0, NODES // 32, normalize, 0, unroll=8)
    bucket(dmean, send_r)
    exchange(send_r, recv_r, 1, 0)
    recv_r[me] = send_r[me]

    def turn(source, out):
        def body(i, carry):
            out[chunk(i, 128), :] = jnp.transpose(source[:, chunk(i, 128)])
            return carry

        lax.fori_loop(0, FF // 128, body, 0)

    loads[6].wait()
    turn(wd, wdt)
    loads[7].wait()
    turn(wg, wgt)
    loads[8].wait()
    turn(wu, wut)

    def flat(ref):
        return ref[...].reshape(ROWS, D)

    def mod(i):
        return lax.rem(i + 2 * REPS, REPS)

    def parts(i):
        low = mod(rep - 1 - i) * SLICE
        high = mod(rep + 1 + i) * SLICE + PART
        return [pl.ds(pl.multiple_of(x, PART), PART) for x in (low, high)]

    def item_rows(i, ref):
        low, high = parts(i)
        return jnp.concatenate([ref[low, :], ref[high, :]], axis=0)

    def hop(d, k, j):
        source = partial.at[0, j, d] if k == 0 else ring.at[k - 1, j, d]
        return pltpu.make_async_remote_copy(
            source, ring.at[k, j, d], ring_send.at[k, j, d], ring_recv.at[k, j, d],
            device_id=(me, rep_up if d == 0 else rep_down), device_id_type=MESH,
        )

    def item_back(i):
        bh_s[...] = dot_last(item_rows(i, wdt), flat(recv_g))

    def item(i, back=True):
        gate_s[...] = dot_last(item_rows(i, wgt), flat(recv_r))
        up_s[...] = dot_last(item_rows(i, wut), flat(recv_r))
        if back:
            item_back(i)
        for d, units in enumerate(parts(i)):

            def act(n, carry):
                rows = pl.ds(pl.multiple_of(d * PART + n * 16, 16), 16)
                here = pl.ds(pl.multiple_of(units.start + n * 16, 16), 16)
                g, u, b = gate_s[rows, :], up_s[rows, :], bh_s[rows, :]
                s = jax.nn.sigmoid(g)
                silu = g * s
                hid_t[here, :] = (silu * u).astype(BF16)
                dgate_t[here, :] = (b * u * s * (1.0 + g * (1.0 - s))).astype(BF16)
                dup_t[here, :] = (b * silu).astype(BF16)
                return carry

            lax.fori_loop(0, PART // 16, act, 0, unroll=6 if i == 0 else 2)
        for j, (left, right) in enumerate(((hid_t, recv_g), (dgate_t, recv_r), (dup_t, recv_r))):
            g = dot(item_rows(i, left), flat(right)).astype(BF16)
            for d in range(2):
                partial[i, j, d] = g[d * PART : (d + 1) * PART, :]
            if i == 0:
                for d in range(2):
                    hop(d, 0, j).start()

    def serve(k, j):
        for d in range(2):
            hop(d, k - 1, j).wait_recv()

            def add(i, carry):
                at = chunk(i, 16)
                ring[k - 1, j, d, at, :] = (
                    ring[k - 1, j, d, at, :].astype(F32) + partial[k, j, d, at, :].astype(F32)
                ).astype(BF16)
                return carry

            lax.fori_loop(0, PART // 16, add, 0, unroll=3)
            hop(d, k, j).start()

    @pl.when(mc == 0)
    def _():
        exchange_wait(recv_g, 0)
        item_back(0)

    for slot, source in enumerate((send_g, send_r)):
        exchange_sent(source, slot, 0)
    exchange(send_g, recv_g, 0, 1)
    exchange(send_r, recv_r, 1, 1)

    @pl.when(mc == 1)
    def _():
        exchange_wait(recv_g, 0)
        item_back(0)

    exchange_wait(recv_r, 1)
    item(0, back=False)
    item(1)
    item(2)
    serve(1, 0)
    serve(1, 1)
    item(3)
    serve(1, 2)
    item(4)
    serve(2, 0)
    item(5)
    serve(2, 1)
    item(6)
    serve(2, 2)
    item(7)
    serve(3, 0)

    def project(terms, out):
        def body(b, carry):
            at = chunk(b, 256)
            y = dot(terms[0][0][at, :], terms[0][1][...])
            for w, x in terms[1:]:
                y = y + dot(w[at, :], x[...])
            out[:, :, at] = jnp.transpose(y).astype(BF16).reshape(EXPERTS, CAP, 256)
            return carry

        lax.fori_loop(0, D // 256, body, 0)

    project(((wd, hid_t),), back_e)
    for core in range(2):
        exchange(back_e, ret_e, 2, core)
    ret_e[me] = back_e[me]
    serve(3, 1)
    project(((wg, dgate_t), (wu, dup_t)), back_d)
    for core in range(2):
        exchange(back_d, ret_d, 3, core)
    ret_d[me] = back_d[me]
    serve(3, 2)
    serve(4, 0)
    rank_col = jnp.sum(jnp.where(same & (second < first), 1.0, 0.0), axis=1, keepdims=True)
    slot_col = (code_col * CAP + rank_col).astype(jnp.int32)
    place[...] = jnp.where(
        lax.broadcasted_iota(jnp.int32, (NODES, ROWS), 1) == slot_col, 1.0, 0.0
    ).astype(BF16)
    counts_t[...] = jnp.transpose(counts[...].astype(F32)).astype(BF16)
    serve(4, 1)
    serve(4, 2)
    for j in range(3):
        serve(5, j)

    exchange_wait(ret_e, 2)
    total[...] = dot(place[...], flat(ret_e))

    def forward_out(i, carry):
        at = chunk(i, 32)
        layer_out[at, :] = (nodes[at, :].astype(F32) + total[at, :]).astype(BF16)
        return carry

    lax.fori_loop(0, NODES // 32, forward_out, 0)
    exchange_wait(ret_d, 3)
    total[...] = dot(place[...], flat(ret_d))

    def norm_back(i, carry):
        at = chunk(i, 32)
        d_norm = total[at, :] * gain_row
        norm = normal[at, :]
        d_mixed = scale_s[at, :] * (d_norm - norm * jnp.mean(d_norm * norm, axis=1, keepdims=True))
        dmean[at, :] = (d_mixed * inv_s[at, :]).astype(BF16)
        total[at, :] = d_out[at, :].astype(F32) + d_mixed
        return carry

    lax.fori_loop(0, NODES // 32, norm_back, 0, unroll=4)
    rim_out[...] = dot(counts_t[pl.ds(NODES, 2 * RIM), :], dmean[...]).astype(BF16)
    rim_last = rim_copies(rim_out.at[pl.ds(RIM, RIM)], rim_out.at[pl.ds(0, RIM)], rim_back, 2)
    for copy in rim_last:
        copy.start()
    serve(6, 0)
    total[...] += dot(counts_t[pl.ds(0, NODES), :], dmean[...])
    serve(6, 1)
    serve(6, 2)
    for copy in rim_last:
        copy.wait_recv()
    total[pl.ds(0, RIM), :] += rim_back[pl.ds(RIM, RIM), :].astype(F32)
    total[pl.ds(NODES - RIM, RIM), :] += rim_back[pl.ds(0, RIM), :].astype(F32)

    def node_out(i, carry):
        at = chunk(i, 32)
        d_nodes[at, :] = total[at, :].astype(BF16)
        return carry

    lax.fori_loop(0, NODES // 32, node_out, 0)
    for copy in rim_first + rim_last:
        copy.wait_send()
    for slot, source in enumerate((send_g, send_r, back_e, back_d)):
        for core in range(2):
            if slot > 1 or core == 1:
                exchange_sent(source, slot, core)
        part = source.at[0]
        pltpu.make_async_copy(part, part, a2a_send.at[slot, 2]).wait()
    for k in range(REPS - 2):
        for j in range(3):
            for d in range(2):
                hop(d, k, j).wait_send()

    for j, out in enumerate((grad_down, grad_gate, grad_up)):
        for d in range(2):
            hop(d, 6, j).wait_recv()

            def last(i, carry):
                at = chunk(i, 16)
                out[pl.ds(pl.multiple_of(d * PART + i * 16, 16), 16), :] = (
                    ring[6, j, d, at, :].astype(F32) + partial[7, j, d, at, :].astype(F32)
                )
                return carry

            lax.fori_loop(0, PART // 16, last, 0, unroll=6)
    for j in range(3):
        for d in range(2):
            hop(d, 6, j).wait_send()


def finish(*refs):
    count = (len(refs) - 1) // 2
    copies = [
        pltpu.make_async_copy(refs[i], refs[count + i], refs[-1].at[i]) for i in range(count)
    ]
    for copy in copies:
        copy.start()
    for copy in copies:
        copy.wait()


def on_device(node_feats, edge_src, edge_dst, node_codes, norm_gain, w_gate, w_up, w_down_t, d_out):
    hbm = pl.BlockSpec(memory_space=pl.ANY)
    vmem = pltpu.VMEM
    sem = pltpu.SemaphoreType.DMA
    weight = vmem((D, FF), BF16)
    weight_t = vmem((FF, D), BF16)
    buckets = vmem((EXPERTS, CAP, D), BF16)
    act_t = vmem((FF, ROWS), BF16)
    rows = vmem((NODES, D), BF16)
    wide = vmem((NODES, D), F32)
    item = vmem((SLICE, ROWS), F32)
    rims = vmem((2 * RIM, D), BF16)
    outs = [jax.ShapeDtypeStruct((NODES, D), BF16)] * 2 + [
        jax.ShapeDtypeStruct((SLICE, D), F32)
    ] * 3
    out = pl.pallas_call(
        kernel,
        out_shape=[vmem(x.shape, x.dtype) for x in outs],
        in_specs=[hbm] * 9,
        out_specs=[pl.BlockSpec(memory_space=vmem)] * 5,
        scratch_shapes=[
            rows,
            vmem((1, EDGES), jnp.int32),
            vmem((1, EDGES), jnp.int32),
            vmem((1, NODES), jnp.int32),
            vmem((D,), F32),
            rows,
        ]
        + [weight] * 3
        + [weight_t] * 3
        + [vmem((REPS, 3, 2, PART, D), BF16), vmem((REPS - 1, 3, 2, PART, D), BF16)]
        + [buckets] * 8
        + [act_t] * 3
        + [item] * 3
        + [
            wide,
            wide,
            vmem((NODES, EXTENT), BF16),
            vmem((EXTENT, NODES), BF16),
            vmem((NODES, ROWS), BF16),
            vmem((ROWS, NODES), BF16),
            vmem((NODES, 1), F32),
            vmem((NODES, 1), F32),
        ]
        + [rims] * 3
        + [
            rows,
            sem((9,)),
            sem((4,)),
            sem((4,)),
            sem((4, 3)),
            sem((4,)),
            sem((REPS - 1, 3, 2)),
            sem((REPS - 1, 3, 2)),
        ],
        compiler_params=pltpu.CompilerParams(
            collective_id=0, has_side_effects=True, vmem_limit_bytes=58 * 2**20
        ),
        name="graph_moe",
    )(
        node_feats[0], edge_src, edge_dst, node_codes.reshape(1, NODES), norm_gain,
        w_gate[0], w_up[0], w_down_t[0], d_out[0],
    )
    layer_out, d_nodes, *grads = pl.pallas_call(
        finish,
        out_shape=outs,
        in_specs=[pl.BlockSpec(memory_space=vmem)] * 5,
        out_specs=[hbm] * 5,
        scratch_shapes=[sem((5,))],
        name="results",
    )(*(pltpu.with_memory_space_constraint(x, pltpu.VMEM) for x in out))
    return (layer_out[None], d_nodes[None], *(g.T[None] for g in grads))


def solution(mesh):
    rows = P("rep", "expert", None)
    edges = P("rep", "expert")
    weights = P("expert", None, None)
    grads = P("expert", None, "rep")
    return jax.shard_map(
        on_device,
        mesh=mesh,
        in_specs=(rows, edges, edges, rows, P(), weights, weights, weights, rows),
        out_specs=(rows, rows, grads, grads, grads),
        check_vma=False,
    )
```

```python
import jax
import jax.numpy as jnp
from jax import lax
from jax.experimental import pallas as pl
from jax.experimental.pallas import tpu as pltpu
from jax.sharding import PartitionSpec as P

MESH = pl.DeviceIdType.MESH
F32 = jnp.float32
BF16 = jnp.bfloat16

D = 768
FF = 1536
NODES = 256
RIM = 64
EXTENT = NODES + 2 * RIM
EDGES = 1024
EXPERTS = 32
CAP = 16
ROWS = EXPERTS * CAP
REPS = 8
SLICE = FF // REPS
PART = SLICE // 2
EARLY, LATE = 1, 0


def partner_order():
    hops = (0, 1, 2, 1)
    offsets = [(a, b) for a in range(4) for b in range(4)][1:]
    offsets.sort(key=lambda o: -(hops[o[0]] + hops[o[1]]))
    order = []
    for a, b in offsets:
        for p in ((a, b), ((4 - a) % 4, (4 - b) % 4)):
            if p not in order:
                order.append(p)
    return order


ORDER = partner_order()
CHIPS = len(ORDER)


def dot(a, b):
    return jnp.dot(a, b, preferred_element_type=F32)


def dot_last(a, b):
    return lax.dot_general(a, b, (((1,), (1,)), ((), ())), preferred_element_type=F32)


def chunk(i, size):
    return pl.ds(pl.multiple_of(i * size, size), size)


def kernel(
    nodes_hbm, sources_hbm, targets_hbm, codes_hbm, gain_hbm, w_gate, w_up, w_down, d_out_hbm,
    layer_out, d_nodes, grad_gate, grad_up, grad_down,
    nodes, sources, targets, codes, gain, d_out,
    wg, wu, wd, wgt, wut, wdt, partial, ring,
    send_g, send_r, recv_g, recv_r, back_e, back_d, ret_e, ret_d,
    hid_t, dgate_t, dup_t, bh_s, gate_s, up_s,
    normal, total, counts, counts_t, place, place_t, scale_s, inv_s,
    rim_in, rim_out, rim_back, dmean,
    load_sem, rim_send, rim_recv, a2a_send, a2a_recv, ring_send, ring_recv,
):
    me = lax.axis_index("expert")
    rep = lax.axis_index("rep")
    my, mx, mc = me // 8, lax.rem(me // 2, 4), lax.rem(me, 2)
    following, before = lax.rem(me + 1, EXPERTS), lax.rem(me + EXPERTS - 1, EXPERTS)
    rep_up, rep_down = lax.rem(rep + 1, REPS), lax.rem(rep + REPS - 1, REPS)

    pairs = (
        (codes_hbm, codes), (d_out_hbm, d_out), (sources_hbm, sources), (targets_hbm, targets),
        (nodes_hbm, nodes), (gain_hbm, gain), (w_down, wd), (w_gate, wg), (w_up, wu),
    )
    loads = [pltpu.make_async_copy(x, y, load_sem.at[i]) for i, (x, y) in enumerate(pairs)]
    for n in (0, 1, 4):
        loads[n].start()

    barrier = pltpu.get_barrier_semaphore()

    def greet(i, carry):
        pl.semaphore_signal(
            barrier, inc=1, device_id=(lax.rem(me + i, EXPERTS), rep), device_id_type=MESH
        )
        return carry

    lax.fori_loop(1, EXPERTS, greet, 0)
    for z in (rep_up, rep_down):
        pl.semaphore_signal(barrier, inc=1, device_id=(me, z), device_id_type=MESH)
    for n in (2, 3, 5, 6, 7, 8):
        loads[n].start()

    loads[0].wait()
    code_row = codes[...].astype(F32)
    code_col = jnp.transpose(jnp.broadcast_to(code_row, (128, NODES)))[:, :1]
    first = lax.broadcasted_iota(jnp.int32, (NODES, NODES), 0)
    second = lax.broadcasted_iota(jnp.int32, (NODES, NODES), 1)
    same = code_col == code_row
    rank_row = jnp.sum(jnp.where(same & (first < second), 1.0, 0.0), axis=0, keepdims=True)
    slot_row = (code_row * CAP + rank_row).astype(jnp.int32)
    place_t[...] = jnp.where(
        lax.broadcasted_iota(jnp.int32, (ROWS, NODES), 0) == slot_row, 1.0, 0.0
    ).astype(BF16)

    def bucket(rows, out):
        out[...] = dot(place_t[...], rows[...]).astype(BF16).reshape(EXPERTS, CAP, D)

    loads[1].wait()
    bucket(d_out, send_g)
    loads[4].wait()
    pl.semaphore_wait(barrier, EXPERTS + 1)

    def rim_copies(low, high, landing, base):
        return [
            pltpu.make_async_remote_copy(
                low, landing.at[pl.ds(0, RIM)], rim_send.at[base], rim_recv.at[base],
                device_id=(before, rep), device_id_type=MESH,
            ),
            pltpu.make_async_remote_copy(
                high, landing.at[pl.ds(RIM, RIM)], rim_send.at[base + 1], rim_recv.at[base + 1],
                device_id=(following, rep), device_id_type=MESH,
            ),
        ]

    rim_first = rim_copies(nodes.at[pl.ds(0, RIM)], nodes.at[pl.ds(NODES - RIM, RIM)], rim_in, 0)
    for copy in rim_first:
        copy.start()

    def exchange(source, landing, slot, core):
        def send(t, sem):
            pltpu.make_async_remote_copy(
                source.at[t], landing.at[me], sem, a2a_recv.at[slot],
                device_id=(t, rep), device_id_type=MESH,
            ).start()

        for a, b in ORDER:
            chip = lax.rem(my + a, 4) * 4 + lax.rem(mx + b, 4)
            send(chip * 2 + core, a2a_send.at[slot, core])

        @pl.when(mc != core)
        def _():
            send(my * 8 + mx * 2 + core, a2a_send.at[slot, 2])

    def exchange_wait(landing, slot):
        part = landing.at[pl.ds(0, EXPERTS - 1)]
        pltpu.make_async_copy(part, part, a2a_recv.at[slot]).wait()

    def exchange_sent(source, slot, core):
        part = source.at[pl.ds(0, CHIPS)]
        pltpu.make_async_copy(part, part, a2a_send.at[slot, core]).wait()

    exchange(send_g, recv_g, 0, EARLY)
    recv_g[me] = send_g[me]

    loads[2].wait()
    loads[3].wait()
    src = sources[...]
    src = jnp.where(src >= RIM, src - RIM, src + (EXTENT - RIM))
    source_hot = jnp.where(
        lax.broadcasted_iota(jnp.int32, (EXTENT, EDGES), 0) == src, 1.0, 0.0
    ).astype(BF16)
    target_hot = jnp.where(
        lax.broadcasted_iota(jnp.int32, (NODES, EDGES), 0) == targets[...], 1.0, 0.0
    ).astype(BF16)
    count = dot_last(target_hot, source_hot)
    counts[...] = count.astype(BF16)
    inv_s[...] = 1.0 / jnp.maximum(jnp.sum(count, axis=1, keepdims=True), 1.0)
    total[...] = dot(counts[:, pl.ds(0, NODES)], nodes[...])
    loads[5].wait()
    for copy in rim_first:
        copy.wait_recv()
    total[...] += dot(counts[:, pl.ds(NODES, 2 * RIM)], rim_in[...])
    gain_row = gain[...].reshape(1, D)

    def normalize(i, carry):
        at = chunk(i, 32)
        mixed = nodes[at, :].astype(F32) + total[at, :] * inv_s[at, :]
        scaling = lax.rsqrt(jnp.mean(mixed * mixed, axis=1, keepdims=True) + 1e-05)
        scale_s[at, :] = scaling
        norm = mixed * scaling
        normal[at, :] = norm
        dmean[at, :] = (norm * gain_row).astype(BF16)
        return carry

    lax.fori_loop(0, NODES // 32, normalize, 0, unroll=8)
    bucket(dmean, send_r)
    exchange(send_r, recv_r, 1, EARLY)
    recv_r[me] = send_r[me]

    def turn(source, out):
        def body(i, carry):
            out[chunk(i, 128), :] = jnp.transpose(source[:, chunk(i, 128)])
            return carry

        lax.fori_loop(0, FF // 128, body, 0)

    loads[6].wait()
    turn(wd, wdt)
    loads[7].wait()
    turn(wg, wgt)
    loads[8].wait()
    turn(wu, wut)

    def flat(ref):
        return ref[...].reshape(ROWS, D)

    def mod(i):
        return lax.rem(i + 2 * REPS, REPS)

    def parts(i):
        low = mod(rep - 1 - i) * SLICE
        high = mod(rep + 1 + i) * SLICE + PART
        return [pl.ds(pl.multiple_of(x, PART), PART) for x in (low, high)]

    def item_rows(i, ref):
        low, high = parts(i)
        return jnp.concatenate([ref[low, :], ref[high, :]], axis=0)

    def hop(d, k, j):
        source = partial.at[0, j, d] if k == 0 else ring.at[k - 1, j, d]
        return pltpu.make_async_remote_copy(
            source, ring.at[k, j, d], ring_send.at[k, j, d], ring_recv.at[k, j, d],
            device_id=(me, rep_up if d == 0 else rep_down), device_id_type=MESH,
        )

    def item_back(i):
        bh_s[...] = dot_last(item_rows(i, wdt), flat(recv_g))

    def item(i, back=True):
        gate_s[...] = dot_last(item_rows(i, wgt), flat(recv_r))
        up_s[...] = dot_last(item_rows(i, wut), flat(recv_r))
        if back:
            item_back(i)
        for d, units in enumerate(parts(i)):

            def act(n, carry):
                rows = pl.ds(pl.multiple_of(d * PART + n * 16, 16), 16)
                here = pl.ds(pl.multiple_of(units.start + n * 16, 16), 16)
                g, u, b = gate_s[rows, :], up_s[rows, :], bh_s[rows, :]
                s = jax.nn.sigmoid(g)
                silu = g * s
                hid_t[here, :] = (silu * u).astype(BF16)
                dgate_t[here, :] = (b * u * s * (1.0 + g * (1.0 - s))).astype(BF16)
                dup_t[here, :] = (b * silu).astype(BF16)
                return carry

            lax.fori_loop(0, PART // 16, act, 0, unroll=6 if i == 0 else 2)
        for j, (left, right) in enumerate(((hid_t, recv_g), (dgate_t, recv_r), (dup_t, recv_r))):
            g = dot(item_rows(i, left), flat(right)).astype(BF16)
            for d in range(2):
                partial[i, j, d] = g[d * PART : (d + 1) * PART, :]
            if i == 0:
                for d in range(2):
                    hop(d, 0, j).start()

    def serve(k, j):
        for d in range(2):
            hop(d, k - 1, j).wait_recv()

            def add(i, carry):
                at = chunk(i, 16)
                ring[k - 1, j, d, at, :] = (
                    ring[k - 1, j, d, at, :].astype(F32) + partial[k, j, d, at, :].astype(F32)
                ).astype(BF16)
                return carry

            lax.fori_loop(0, PART // 16, add, 0, unroll=3)
            hop(d, k, j).start()

    @pl.when(mc == EARLY)
    def _():
        exchange_wait(recv_g, 0)
        item_back(0)

    for slot, source in enumerate((send_g, send_r)):
        exchange_sent(source, slot, EARLY)
    exchange(send_g, recv_g, 0, LATE)
    exchange(send_r, recv_r, 1, LATE)

    @pl.when(mc == LATE)
    def _():
        exchange_wait(recv_g, 0)
        item_back(0)

    exchange_wait(recv_r, 1)
    item(0, back=False)
    item(1)
    item(2)
    serve(1, 0)
    serve(1, 1)
    item(3)
    serve(1, 2)
    item(4)
    serve(2, 0)
    item(5)
    serve(2, 1)
    item(6)
    serve(2, 2)
    item(7)
    serve(3, 0)

    def project(terms, out):
        def body(b, carry):
            at = chunk(b, 256)
            y = dot(terms[0][0][at, :], terms[0][1][...])
            for w, x in terms[1:]:
                y = y + dot(w[at, :], x[...])
            out[:, :, at] = jnp.transpose(y).astype(BF16).reshape(EXPERTS, CAP, 256)
            return carry

        lax.fori_loop(0, D // 256, body, 0)

    project(((wd, hid_t),), back_e)
    for core in range(2):
        exchange(back_e, ret_e, 2, core)
    ret_e[me] = back_e[me]
    serve(3, 1)
    project(((wg, dgate_t), (wu, dup_t)), back_d)
    for core in range(2):
        exchange(back_d, ret_d, 3, core)
    ret_d[me] = back_d[me]
    serve(3, 2)
    serve(4, 0)
    rank_col = jnp.sum(jnp.where(same & (second < first), 1.0, 0.0), axis=1, keepdims=True)
    slot_col = (code_col * CAP + rank_col).astype(jnp.int32)
    place[...] = jnp.where(
        lax.broadcasted_iota(jnp.int32, (NODES, ROWS), 1) == slot_col, 1.0, 0.0
    ).astype(BF16)
    counts_t[...] = jnp.transpose(counts[...].astype(F32)).astype(BF16)
    serve(4, 1)
    serve(4, 2)
    for j in range(3):
        serve(5, j)

    exchange_wait(ret_e, 2)
    total[...] = dot(place[...], flat(ret_e))

    def forward_out(i, carry):
        at = chunk(i, 32)
        layer_out[at, :] = (nodes[at, :].astype(F32) + total[at, :]).astype(BF16)
        return carry

    lax.fori_loop(0, NODES // 32, forward_out, 0)
    exchange_wait(ret_d, 3)
    total[...] = dot(place[...], flat(ret_d))

    def norm_back(i, carry):
        at = chunk(i, 32)
        d_norm = total[at, :] * gain_row
        norm = normal[at, :]
        d_mixed = scale_s[at, :] * (d_norm - norm * jnp.mean(d_norm * norm, axis=1, keepdims=True))
        dmean[at, :] = (d_mixed * inv_s[at, :]).astype(BF16)
        total[at, :] = d_out[at, :].astype(F32) + d_mixed
        return carry

    lax.fori_loop(0, NODES // 32, norm_back, 0, unroll=4)
    rim_out[...] = dot(counts_t[pl.ds(NODES, 2 * RIM), :], dmean[...]).astype(BF16)
    rim_last = rim_copies(rim_out.at[pl.ds(RIM, RIM)], rim_out.at[pl.ds(0, RIM)], rim_back, 2)
    for copy in rim_last:
        copy.start()
    serve(6, 0)
    total[...] += dot(counts_t[pl.ds(0, NODES), :], dmean[...])
    serve(6, 1)
    serve(6, 2)
    for copy in rim_last:
        copy.wait_recv()
    total[pl.ds(0, RIM), :] += rim_back[pl.ds(RIM, RIM), :].astype(F32)
    total[pl.ds(NODES - RIM, RIM), :] += rim_back[pl.ds(0, RIM), :].astype(F32)

    def node_out(i, carry):
        at = chunk(i, 32)
        d_nodes[at, :] = total[at, :].astype(BF16)
        return carry

    lax.fori_loop(0, NODES // 32, node_out, 0)
    for copy in rim_first + rim_last:
        copy.wait_send()
    for slot, source in enumerate((send_g, send_r, back_e, back_d)):
        for core in range(2):
            if slot > 1 or core == LATE:
                exchange_sent(source, slot, core)
        part = source.at[0]
        pltpu.make_async_copy(part, part, a2a_send.at[slot, 2]).wait()
    for k in range(REPS - 2):
        for j in range(3):
            for d in range(2):
                hop(d, k, j).wait_send()

    for j, out in enumerate((grad_down, grad_gate, grad_up)):
        for d in range(2):
            hop(d, 6, j).wait_recv()

            def last(i, carry):
                at = chunk(i, 16)
                out[pl.ds(pl.multiple_of(d * PART + i * 16, 16), 16), :] = (
                    ring[6, j, d, at, :].astype(F32) + partial[7, j, d, at, :].astype(F32)
                )
                return carry

            lax.fori_loop(0, PART // 16, last, 0, unroll=6)
    for j in range(3):
        for d in range(2):
            hop(d, 6, j).wait_send()


def finish(*refs):
    count = (len(refs) - 1) // 2
    copies = [
        pltpu.make_async_copy(refs[i], refs[count + i], refs[-1].at[i]) for i in range(count)
    ]
    for copy in copies:
        copy.start()
    for copy in copies:
        copy.wait()


def on_device(node_feats, edge_src, edge_dst, node_codes, norm_gain, w_gate, w_up, w_down_t, d_out):
    hbm = pl.BlockSpec(memory_space=pl.ANY)
    vmem = pltpu.VMEM
    sem = pltpu.SemaphoreType.DMA
    weight = vmem((D, FF), BF16)
    weight_t = vmem((FF, D), BF16)
    buckets = vmem((EXPERTS, CAP, D), BF16)
    act_t = vmem((FF, ROWS), BF16)
    rows = vmem((NODES, D), BF16)
    wide = vmem((NODES, D), F32)
    item = vmem((SLICE, ROWS), F32)
    rims = vmem((2 * RIM, D), BF16)
    outs = [jax.ShapeDtypeStruct((NODES, D), BF16)] * 2 + [
        jax.ShapeDtypeStruct((SLICE, D), F32)
    ] * 3
    out = pl.pallas_call(
        kernel,
        out_shape=[vmem(x.shape, x.dtype) for x in outs],
        in_specs=[hbm] * 9,
        out_specs=[pl.BlockSpec(memory_space=vmem)] * 5,
        scratch_shapes=[
            rows,
            vmem((1, EDGES), jnp.int32),
            vmem((1, EDGES), jnp.int32),
            vmem((1, NODES), jnp.int32),
            vmem((D,), F32),
            rows,
        ]
        + [weight] * 3
        + [weight_t] * 3
        + [vmem((REPS, 3, 2, PART, D), BF16), vmem((REPS - 1, 3, 2, PART, D), BF16)]
        + [buckets] * 8
        + [act_t] * 3
        + [item] * 3
        + [
            wide,
            wide,
            vmem((NODES, EXTENT), BF16),
            vmem((EXTENT, NODES), BF16),
            vmem((NODES, ROWS), BF16),
            vmem((ROWS, NODES), BF16),
            vmem((NODES, 1), F32),
            vmem((NODES, 1), F32),
        ]
        + [rims] * 3
        + [
            rows,
            sem((9,)),
            sem((4,)),
            sem((4,)),
            sem((4, 3)),
            sem((4,)),
            sem((REPS - 1, 3, 2)),
            sem((REPS - 1, 3, 2)),
        ],
        compiler_params=pltpu.CompilerParams(
            collective_id=0, has_side_effects=True, vmem_limit_bytes=58 * 2**20
        ),
        name="graph_moe",
    )(
        node_feats[0], edge_src, edge_dst, node_codes.reshape(1, NODES), norm_gain,
        w_gate[0], w_up[0], w_down_t[0], d_out[0],
    )
    layer_out, d_nodes, *grads = pl.pallas_call(
        finish,
        out_shape=outs,
        in_specs=[pl.BlockSpec(memory_space=vmem)] * 5,
        out_specs=[hbm] * 5,
        scratch_shapes=[sem((5,))],
        name="results",
    )(*(pltpu.with_memory_space_constraint(x, pltpu.VMEM) for x in out))
    return (layer_out[None], d_nodes[None], *(g.T[None] for g in grads))


def solution(mesh):
    rows = P("rep", "expert", None)
    edges = P("rep", "expert")
    weights = P("expert", None, None)
    grads = P("expert", None, "rep")
    return jax.shard_map(
        on_device,
        mesh=mesh,
        in_specs=(rows, edges, edges, rows, P(), weights, weights, weights, rows),
        out_specs=(rows, rows, grads, grads, grads),
        check_vma=False,
    )
```

```python
import jax
import jax.numpy as jnp
from jax import lax
from jax.experimental import pallas as pl
from jax.experimental.pallas import tpu as pltpu
from jax.sharding import PartitionSpec as P

MESH = pl.DeviceIdType.MESH
F32 = jnp.float32
BF16 = jnp.bfloat16

D = 768
FF = 1536
NODES = 256
RIM = 64
EXTENT = NODES + 2 * RIM
EDGES = 1024
EXPERTS = 32
CAP = 16
ROWS = EXPERTS * CAP
REPS = 8
SLICE = FF // REPS
PART = SLICE // 2
EARLY, LATE = 1, 0
GROUP = EXPERTS // 2


def partner_order():
    hops = (0, 1, 2, 1)
    offsets = [(a, b) for a in range(4) for b in range(4)][1:]
    offsets.sort(key=lambda o: -(hops[o[0]] + hops[o[1]]))
    order = []
    for a, b in offsets:
        for p in ((a, b), ((4 - a) % 4, (4 - b) % 4)):
            if p not in order:
                order.append(p)
    return order


ORDER = partner_order()
CHIPS = len(ORDER)


def dot(a, b):
    return jnp.dot(a, b, preferred_element_type=F32)


def dot_last(a, b):
    return lax.dot_general(a, b, (((1,), (1,)), ((), ())), preferred_element_type=F32)


def chunk(i, size):
    return pl.ds(pl.multiple_of(i * size, size), size)


def kernel(
    nodes_hbm, sources_hbm, targets_hbm, codes_hbm, gain_hbm, w_gate, w_up, w_down, d_out_hbm,
    layer_out, d_nodes, grad_gate, grad_up, grad_down,
    nodes, sources, targets, codes, gain, d_out,
    wg, wu, wd, wgt, wut, wdt, partial, ring,
    send_g, send_r, recv_g, recv_r, back_e, back_d, ret_e, ret_d,
    hid_t, dgate_t, dup_t, bh_s, gate_s, up_s,
    normal, total, counts, counts_t, place, place_t, scale_s, inv_s,
    rim_in, rim_out, rim_back, dmean,
    load_sem, rim_send, rim_recv, a2a_send, a2a_recv, ring_send, ring_recv,
):
    me = lax.axis_index("expert")
    rep = lax.axis_index("rep")
    my, mx, mc = me // 8, lax.rem(me // 2, 4), lax.rem(me, 2)
    following, before = lax.rem(me + 1, EXPERTS), lax.rem(me + EXPERTS - 1, EXPERTS)
    rep_up, rep_down = lax.rem(rep + 1, REPS), lax.rem(rep + REPS - 1, REPS)

    pairs = (
        (codes_hbm, codes), (d_out_hbm, d_out), (sources_hbm, sources), (targets_hbm, targets),
        (nodes_hbm, nodes), (gain_hbm, gain), (w_down, wd), (w_gate, wg), (w_up, wu),
    )
    loads = [pltpu.make_async_copy(x, y, load_sem.at[i]) for i, (x, y) in enumerate(pairs)]
    for n in (0, 1, 4):
        loads[n].start()

    barrier = pltpu.get_barrier_semaphore()

    def greet(i, carry):
        pl.semaphore_signal(
            barrier, inc=1, device_id=(lax.rem(me + i, EXPERTS), rep), device_id_type=MESH
        )
        return carry

    lax.fori_loop(1, EXPERTS, greet, 0)
    for z in (rep_up, rep_down):
        pl.semaphore_signal(barrier, inc=1, device_id=(me, z), device_id_type=MESH)
    for n in (2, 3, 5, 6, 7, 8):
        loads[n].start()

    loads[0].wait()
    code_row = codes[...].astype(F32)
    code_col = jnp.transpose(jnp.broadcast_to(code_row, (128, NODES)))[:, :1]
    first = lax.broadcasted_iota(jnp.int32, (NODES, NODES), 0)
    second = lax.broadcasted_iota(jnp.int32, (NODES, NODES), 1)
    same = code_col == code_row
    rank_row = jnp.sum(jnp.where(same & (first < second), 1.0, 0.0), axis=0, keepdims=True)
    code = codes[...]
    group = jnp.where(lax.rem(code, 2) == EARLY, 0, ROWS // 2)
    slot_row = group + lax.div(code, 2) * CAP + rank_row.astype(jnp.int32)
    place_t[...] = jnp.where(
        lax.broadcasted_iota(jnp.int32, (ROWS, NODES), 0) == slot_row, 1.0, 0.0
    ).astype(BF16)

    def bucket(rows, out, core):
        half = 0 if core == EARLY else 1
        filled = dot(place_t[pl.ds(half * (ROWS // 2), ROWS // 2), :], rows[...]).astype(BF16)
        out[pl.ds(half * GROUP, GROUP)] = filled.reshape(GROUP, CAP, D)

    loads[1].wait()
    bucket(d_out, send_g, EARLY)
    bucket(d_out, send_g, LATE)
    loads[4].wait()
    pl.semaphore_wait(barrier, EXPERTS + 1)

    def rim_copies(low, high, landing, base):
        return [
            pltpu.make_async_remote_copy(
                low, landing.at[pl.ds(0, RIM)], rim_send.at[base], rim_recv.at[base],
                device_id=(before, rep), device_id_type=MESH,
            ),
            pltpu.make_async_remote_copy(
                high, landing.at[pl.ds(RIM, RIM)], rim_send.at[base + 1], rim_recv.at[base + 1],
                device_id=(following, rep), device_id_type=MESH,
            ),
        ]

    rim_first = rim_copies(nodes.at[pl.ds(0, RIM)], nodes.at[pl.ds(NODES - RIM, RIM)], rim_in, 0)
    for copy in rim_first:
        copy.start()

    def exchange(source, landing, slot, core):
        def send(chip, sem):
            t = chip * 2 + core
            from_ = t if slot > 1 else chip + (0 if core == EARLY else GROUP)
            pltpu.make_async_remote_copy(
                source.at[from_], landing.at[me], sem, a2a_recv.at[slot],
                device_id=(t, rep), device_id_type=MESH,
            ).start()

        for a, b in ORDER:
            chip = lax.rem(my + a, 4) * 4 + lax.rem(mx + b, 4)
            send(chip, a2a_send.at[slot, core])

        @pl.when(mc != core)
        def _():
            send(my * 4 + mx, a2a_send.at[slot, 2])

    def exchange_wait(landing, slot):
        part = landing.at[pl.ds(0, EXPERTS - 1)]
        pltpu.make_async_copy(part, part, a2a_recv.at[slot]).wait()

    def exchange_sent(source, slot, core):
        part = source.at[pl.ds(0, CHIPS)]
        pltpu.make_async_copy(part, part, a2a_send.at[slot, core]).wait()

    exchange(send_g, recv_g, 0, EARLY)
    own = jnp.where(mc == EARLY, 0, GROUP) + my * 4 + mx
    recv_g[me] = send_g[own]

    loads[2].wait()
    loads[3].wait()
    src = sources[...]
    src = jnp.where(src >= RIM, src - RIM, src + (EXTENT - RIM))
    source_hot = jnp.where(
        lax.broadcasted_iota(jnp.int32, (EXTENT, EDGES), 0) == src, 1.0, 0.0
    ).astype(BF16)
    target_hot = jnp.where(
        lax.broadcasted_iota(jnp.int32, (NODES, EDGES), 0) == targets[...], 1.0, 0.0
    ).astype(BF16)
    count = dot_last(target_hot, source_hot)
    counts[...] = count.astype(BF16)
    inv_s[...] = 1.0 / jnp.maximum(jnp.sum(count, axis=1, keepdims=True), 1.0)
    total[...] = dot(counts[:, pl.ds(0, NODES)], nodes[...])
    loads[5].wait()
    for copy in rim_first:
        copy.wait_recv()
    total[...] += dot(counts[:, pl.ds(NODES, 2 * RIM)], rim_in[...])
    gain_row = gain[...].reshape(1, D)

    def normalize(i, carry):
        at = chunk(i, 32)
        mixed = nodes[at, :].astype(F32) + total[at, :] * inv_s[at, :]
        scaling = lax.rsqrt(jnp.mean(mixed * mixed, axis=1, keepdims=True) + 1e-05)
        scale_s[at, :] = scaling
        norm = mixed * scaling
        normal[at, :] = norm
        dmean[at, :] = (norm * gain_row).astype(BF16)
        return carry

    lax.fori_loop(0, NODES // 32, normalize, 0, unroll=8)
    bucket(dmean, send_r, EARLY)
    exchange(send_r, recv_r, 1, EARLY)
    bucket(dmean, send_r, LATE)
    recv_r[me] = send_r[own]

    def turn(source, out):
        def body(i, carry):
            out[chunk(i, 128), :] = jnp.transpose(source[:, chunk(i, 128)])
            return carry

        lax.fori_loop(0, FF // 128, body, 0)

    loads[6].wait()
    turn(wd, wdt)
    loads[7].wait()
    turn(wg, wgt)
    loads[8].wait()
    turn(wu, wut)

    def flat(ref):
        return ref[...].reshape(ROWS, D)

    def mod(i):
        return lax.rem(i + 2 * REPS, REPS)

    def parts(i):
        low = mod(rep - 1 - i) * SLICE
        high = mod(rep + 1 + i) * SLICE + PART
        return [pl.ds(pl.multiple_of(x, PART), PART) for x in (low, high)]

    def item_rows(i, ref):
        low, high = parts(i)
        return jnp.concatenate([ref[low, :], ref[high, :]], axis=0)

    def hop(d, k, j):
        source = partial.at[0, j, d] if k == 0 else ring.at[k - 1, j, d]
        return pltpu.make_async_remote_copy(
            source, ring.at[k, j, d], ring_send.at[k, j, d], ring_recv.at[k, j, d],
            device_id=(me, rep_up if d == 0 else rep_down), device_id_type=MESH,
        )

    def item_back(i):
        bh_s[...] = dot_last(item_rows(i, wdt), flat(recv_g))

    def item(i, back=True):
        gate_s[...] = dot_last(item_rows(i, wgt), flat(recv_r))
        up_s[...] = dot_last(item_rows(i, wut), flat(recv_r))
        if back:
            item_back(i)
        for d, units in enumerate(parts(i)):

            def act(n, carry):
                rows = pl.ds(pl.multiple_of(d * PART + n * 16, 16), 16)
                here = pl.ds(pl.multiple_of(units.start + n * 16, 16), 16)
                g, u, b = gate_s[rows, :], up_s[rows, :], bh_s[rows, :]
                s = jax.nn.sigmoid(g)
                silu = g * s
                hid_t[here, :] = (silu * u).astype(BF16)
                dgate_t[here, :] = (b * u * s * (1.0 + g * (1.0 - s))).astype(BF16)
                dup_t[here, :] = (b * silu).astype(BF16)
                return carry

            lax.fori_loop(0, PART // 16, act, 0, unroll=6 if i == 0 else 2)
        for j, (left, right) in enumerate(((hid_t, recv_g), (dgate_t, recv_r), (dup_t, recv_r))):
            g = dot(item_rows(i, left), flat(right)).astype(BF16)
            for d in range(2):
                partial[i, j, d] = g[d * PART : (d + 1) * PART, :]
            if i == 0:
                for d in range(2):
                    hop(d, 0, j).start()

    def serve(k, j):
        for d in range(2):
            hop(d, k - 1, j).wait_recv()

            def add(i, carry):
                at = chunk(i, 16)
                ring[k - 1, j, d, at, :] = (
                    ring[k - 1, j, d, at, :].astype(F32) + partial[k, j, d, at, :].astype(F32)
                ).astype(BF16)
                return carry

            lax.fori_loop(0, PART // 16, add, 0, unroll=3)
            hop(d, k, j).start()

    @pl.when(mc == EARLY)
    def _():
        exchange_wait(recv_g, 0)
        item_back(0)

    for slot, source in enumerate((send_g, send_r)):
        exchange_sent(source, slot, EARLY)
    exchange(send_g, recv_g, 0, LATE)
    exchange(send_r, recv_r, 1, LATE)

    @pl.when(mc == LATE)
    def _():
        exchange_wait(recv_g, 0)
        item_back(0)

    exchange_wait(recv_r, 1)
    item(0, back=False)
    item(1)
    item(2)
    serve(1, 0)
    serve(1, 1)
    item(3)
    serve(1, 2)
    item(4)
    serve(2, 0)
    item(5)
    serve(2, 1)
    item(6)
    serve(2, 2)
    item(7)
    serve(3, 0)

    def project(terms, out):
        def body(b, carry):
            at = chunk(b, 256)
            y = dot(terms[0][0][at, :], terms[0][1][...])
            for w, x in terms[1:]:
                y = y + dot(w[at, :], x[...])
            out[:, :, at] = jnp.transpose(y).astype(BF16).reshape(EXPERTS, CAP, 256)
            return carry

        lax.fori_loop(0, D // 256, body, 0)

    project(((wd, hid_t),), back_e)
    for core in range(2):
        exchange(back_e, ret_e, 2, core)
    ret_e[me] = back_e[me]
    serve(3, 1)
    project(((wg, dgate_t), (wu, dup_t)), back_d)
    for core in range(2):
        exchange(back_d, ret_d, 3, core)
    ret_d[me] = back_d[me]
    serve(3, 2)
    serve(4, 0)
    rank_col = jnp.sum(jnp.where(same & (second < first), 1.0, 0.0), axis=1, keepdims=True)
    slot_col = (code_col * CAP + rank_col).astype(jnp.int32)
    place[...] = jnp.where(
        lax.broadcasted_iota(jnp.int32, (NODES, ROWS), 1) == slot_col, 1.0, 0.0
    ).astype(BF16)
    counts_t[...] = jnp.transpose(counts[...].astype(F32)).astype(BF16)
    serve(4, 1)
    serve(4, 2)
    for j in range(3):
        serve(5, j)

    exchange_wait(ret_e, 2)
    total[...] = dot(place[...], flat(ret_e))

    def forward_out(i, carry):
        at = chunk(i, 32)
        layer_out[at, :] = (nodes[at, :].astype(F32) + total[at, :]).astype(BF16)
        return carry

    lax.fori_loop(0, NODES // 32, forward_out, 0)
    exchange_wait(ret_d, 3)
    total[...] = dot(place[...], flat(ret_d))

    def norm_back(i, carry):
        at = chunk(i, 32)
        d_norm = total[at, :] * gain_row
        norm = normal[at, :]
        d_mixed = scale_s[at, :] * (d_norm - norm * jnp.mean(d_norm * norm, axis=1, keepdims=True))
        dmean[at, :] = (d_mixed * inv_s[at, :]).astype(BF16)
        total[at, :] = d_out[at, :].astype(F32) + d_mixed
        return carry

    lax.fori_loop(0, NODES // 32, norm_back, 0, unroll=4)
    rim_out[...] = dot(counts_t[pl.ds(NODES, 2 * RIM), :], dmean[...]).astype(BF16)
    rim_last = rim_copies(rim_out.at[pl.ds(RIM, RIM)], rim_out.at[pl.ds(0, RIM)], rim_back, 2)
    for copy in rim_last:
        copy.start()
    serve(6, 0)
    total[...] += dot(counts_t[pl.ds(0, NODES), :], dmean[...])
    serve(6, 1)
    serve(6, 2)
    for copy in rim_last:
        copy.wait_recv()
    total[pl.ds(0, RIM), :] += rim_back[pl.ds(RIM, RIM), :].astype(F32)
    total[pl.ds(NODES - RIM, RIM), :] += rim_back[pl.ds(0, RIM), :].astype(F32)

    def node_out(i, carry):
        at = chunk(i, 32)
        d_nodes[at, :] = total[at, :].astype(BF16)
        return carry

    lax.fori_loop(0, NODES // 32, node_out, 0)
    for copy in rim_first + rim_last:
        copy.wait_send()
    for slot, source in enumerate((send_g, send_r, back_e, back_d)):
        for core in range(2):
            if slot > 1 or core == LATE:
                exchange_sent(source, slot, core)
        part = source.at[0]
        pltpu.make_async_copy(part, part, a2a_send.at[slot, 2]).wait()
    for k in range(REPS - 2):
        for j in range(3):
            for d in range(2):
                hop(d, k, j).wait_send()

    for j, out in enumerate((grad_down, grad_gate, grad_up)):
        for d in range(2):
            hop(d, 6, j).wait_recv()

            def last(i, carry):
                at = chunk(i, 16)
                out[pl.ds(pl.multiple_of(d * PART + i * 16, 16), 16), :] = (
                    ring[6, j, d, at, :].astype(F32) + partial[7, j, d, at, :].astype(F32)
                )
                return carry

            lax.fori_loop(0, PART // 16, last, 0, unroll=6)
    for j in range(3):
        for d in range(2):
            hop(d, 6, j).wait_send()


def finish(*refs):
    count = (len(refs) - 1) // 2
    copies = [
        pltpu.make_async_copy(refs[i], refs[count + i], refs[-1].at[i]) for i in range(count)
    ]
    for copy in copies:
        copy.start()
    for copy in copies:
        copy.wait()


def on_device(node_feats, edge_src, edge_dst, node_codes, norm_gain, w_gate, w_up, w_down_t, d_out):
    hbm = pl.BlockSpec(memory_space=pl.ANY)
    vmem = pltpu.VMEM
    sem = pltpu.SemaphoreType.DMA
    weight = vmem((D, FF), BF16)
    weight_t = vmem((FF, D), BF16)
    buckets = vmem((EXPERTS, CAP, D), BF16)
    act_t = vmem((FF, ROWS), BF16)
    rows = vmem((NODES, D), BF16)
    wide = vmem((NODES, D), F32)
    item = vmem((SLICE, ROWS), F32)
    rims = vmem((2 * RIM, D), BF16)
    outs = [jax.ShapeDtypeStruct((NODES, D), BF16)] * 2 + [
        jax.ShapeDtypeStruct((SLICE, D), F32)
    ] * 3
    out = pl.pallas_call(
        kernel,
        out_shape=[vmem(x.shape, x.dtype) for x in outs],
        in_specs=[hbm] * 9,
        out_specs=[pl.BlockSpec(memory_space=vmem)] * 5,
        scratch_shapes=[
            rows,
            vmem((1, EDGES), jnp.int32),
            vmem((1, EDGES), jnp.int32),
            vmem((1, NODES), jnp.int32),
            vmem((D,), F32),
            rows,
        ]
        + [weight] * 3
        + [weight_t] * 3
        + [vmem((REPS, 3, 2, PART, D), BF16), vmem((REPS - 1, 3, 2, PART, D), BF16)]
        + [buckets] * 8
        + [act_t] * 3
        + [item] * 3
        + [
            wide,
            wide,
            vmem((NODES, EXTENT), BF16),
            vmem((EXTENT, NODES), BF16),
            vmem((NODES, ROWS), BF16),
            vmem((ROWS, NODES), BF16),
            vmem((NODES, 1), F32),
            vmem((NODES, 1), F32),
        ]
        + [rims] * 3
        + [
            rows,
            sem((9,)),
            sem((4,)),
            sem((4,)),
            sem((4, 3)),
            sem((4,)),
            sem((REPS - 1, 3, 2)),
            sem((REPS - 1, 3, 2)),
        ],
        compiler_params=pltpu.CompilerParams(
            collective_id=0, has_side_effects=True, vmem_limit_bytes=58 * 2**20
        ),
        name="graph_moe",
    )(
        node_feats[0], edge_src, edge_dst, node_codes.reshape(1, NODES), norm_gain,
        w_gate[0], w_up[0], w_down_t[0], d_out[0],
    )
    layer_out, d_nodes, *grads = pl.pallas_call(
        finish,
        out_shape=outs,
        in_specs=[pl.BlockSpec(memory_space=vmem)] * 5,
        out_specs=[hbm] * 5,
        scratch_shapes=[sem((5,))],
        name="results",
    )(*(pltpu.with_memory_space_constraint(x, pltpu.VMEM) for x in out))
    return (layer_out[None], d_nodes[None], *(g.T[None] for g in grads))


def solution(mesh):
    rows = P("rep", "expert", None)
    edges = P("rep", "expert")
    weights = P("expert", None, None)
    grads = P("expert", None, "rep")
    return jax.shard_map(
        on_device,
        mesh=mesh,
        in_specs=(rows, edges, edges, rows, P(), weights, weights, weights, rows),
        out_specs=(rows, rows, grads, grads, grads),
        check_vma=False,
    )
```

```python
import jax
import jax.numpy as jnp
from jax import lax
from jax.experimental import pallas as pl
from jax.experimental.pallas import tpu as pltpu
from jax.sharding import PartitionSpec as P

MESH = pl.DeviceIdType.MESH
F32 = jnp.float32
BF16 = jnp.bfloat16

D = 768
FF = 1536
NODES = 256
RIM = 64
EXTENT = NODES + 2 * RIM
EDGES = 1024
EXPERTS = 32
CAP = 16
ROWS = EXPERTS * CAP
REPS = 8
SLICE = FF // REPS
PART = SLICE // 2
EARLY, LATE = 1, 0
GROUP = EXPERTS // 2


def partner_order():
    hops = (0, 1, 2, 1)
    offsets = [(a, b) for a in range(4) for b in range(4)][1:]
    offsets.sort(key=lambda o: -(hops[o[0]] + hops[o[1]]))
    order = []
    for a, b in offsets:
        for p in ((a, b), ((4 - a) % 4, (4 - b) % 4)):
            if p not in order:
                order.append(p)
    return order


ORDER = partner_order()
CHIPS = len(ORDER)


def dot(a, b):
    return jnp.dot(a, b, preferred_element_type=F32)


def dot_last(a, b):
    return lax.dot_general(a, b, (((1,), (1,)), ((), ())), preferred_element_type=F32)


def chunk(i, size):
    return pl.ds(pl.multiple_of(i * size, size), size)


def kernel(
    nodes_hbm, sources_hbm, targets_hbm, codes_hbm, gain_hbm, w_gate, w_up, w_down, d_out_hbm,
    layer_out, d_nodes, grad_gate, grad_up, grad_down,
    nodes, sources, targets, codes, gain, d_out,
    wg, wu, wd, wgt, wut, wdt, partial, ring,
    send_g, send_r, recv_g, recv_r, back_e, back_d, ret_e, ret_d,
    hid_t, dgate_t, dup_t, bh_s, gate_s, up_s,
    normal, total, counts, counts_t, place, place_t, scale_s, inv_s,
    rim_in, rim_out, rim_back, dmean,
    load_sem, rim_send, rim_recv, a2a_send, a2a_recv, ring_send, ring_recv,
):
    me = lax.axis_index("expert")
    rep = lax.axis_index("rep")
    my, mx, mc = me // 8, lax.rem(me // 2, 4), lax.rem(me, 2)
    following, before = lax.rem(me + 1, EXPERTS), lax.rem(me + EXPERTS - 1, EXPERTS)
    rep_up, rep_down = lax.rem(rep + 1, REPS), lax.rem(rep + REPS - 1, REPS)

    pairs = (
        (codes_hbm, codes), (d_out_hbm, d_out), (sources_hbm, sources), (targets_hbm, targets),
        (nodes_hbm, nodes), (gain_hbm, gain), (w_down, wd), (w_gate, wg), (w_up, wu),
    )
    loads = [pltpu.make_async_copy(x, y, load_sem.at[i]) for i, (x, y) in enumerate(pairs)]
    for n in (0, 1, 4):
        loads[n].start()

    barrier = pltpu.get_barrier_semaphore()

    def greet(i, carry):
        pl.semaphore_signal(
            barrier, inc=1, device_id=(lax.rem(me + i, EXPERTS), rep), device_id_type=MESH
        )
        return carry

    lax.fori_loop(1, EXPERTS, greet, 0)
    for z in (rep_up, rep_down):
        pl.semaphore_signal(barrier, inc=1, device_id=(me, z), device_id_type=MESH)
    for n in (2, 3, 5, 6, 7, 8):
        loads[n].start()

    loads[0].wait()
    code_row = codes[...].astype(F32)
    code_col = jnp.transpose(jnp.broadcast_to(code_row, (128, NODES)))[:, :1]
    first = lax.broadcasted_iota(jnp.int32, (NODES, NODES), 0)
    second = lax.broadcasted_iota(jnp.int32, (NODES, NODES), 1)
    same = code_col == code_row
    rank_row = jnp.sum(jnp.where(same & (first < second), 1.0, 0.0), axis=0, keepdims=True)
    code = codes[...]
    group = jnp.where(lax.rem(code, 2) == EARLY, 0, ROWS // 2)
    slot_row = group + lax.div(code, 2) * CAP + rank_row.astype(jnp.int32)
    place_t[...] = jnp.where(
        lax.broadcasted_iota(jnp.int32, (ROWS, NODES), 0) == slot_row, 1.0, 0.0
    ).astype(BF16)

    def bucket(rows, out, core):
        half = 0 if core == EARLY else 1
        filled = dot(place_t[pl.ds(half * (ROWS // 2), ROWS // 2), :], rows[...]).astype(BF16)
        out[pl.ds(half * GROUP, GROUP)] = filled.reshape(GROUP, CAP, D)

    loads[1].wait()
    bucket(d_out, send_g, EARLY)
    bucket(d_out, send_g, LATE)
    loads[4].wait()
    pl.semaphore_wait(barrier, EXPERTS + 1)

    def rim_copies(low, high, landing, base):
        return [
            pltpu.make_async_remote_copy(
                low, landing.at[pl.ds(0, RIM)], rim_send.at[base], rim_recv.at[base],
                device_id=(before, rep), device_id_type=MESH,
            ),
            pltpu.make_async_remote_copy(
                high, landing.at[pl.ds(RIM, RIM)], rim_send.at[base + 1], rim_recv.at[base + 1],
                device_id=(following, rep), device_id_type=MESH,
            ),
        ]

    rim_first = rim_copies(nodes.at[pl.ds(0, RIM)], nodes.at[pl.ds(NODES - RIM, RIM)], rim_in, 0)
    for copy in rim_first:
        copy.start()

    def exchange(source, landing, slot, core):
        def send(chip, sem):
            t = chip * 2 + core
            from_ = t if slot > 1 else chip + (0 if core == EARLY else GROUP)
            pltpu.make_async_remote_copy(
                source.at[from_], landing.at[me], sem, a2a_recv.at[slot],
                device_id=(t, rep), device_id_type=MESH,
            ).start()

        for a, b in ORDER:
            chip = lax.rem(my + a, 4) * 4 + lax.rem(mx + b, 4)
            send(chip, a2a_send.at[slot, core])

        @pl.when(mc != core)
        def _():
            send(my * 4 + mx, a2a_send.at[slot, 2])

    def exchange_wait(landing, slot):
        part = landing.at[pl.ds(0, EXPERTS - 1)]
        pltpu.make_async_copy(part, part, a2a_recv.at[slot]).wait()

    def exchange_sent(source, slot, core):
        part = source.at[pl.ds(0, CHIPS)]
        pltpu.make_async_copy(part, part, a2a_send.at[slot, core]).wait()

    exchange(send_g, recv_g, 0, EARLY)
    own = jnp.where(mc == EARLY, 0, GROUP) + my * 4 + mx
    recv_g[me] = send_g[own]

    loads[2].wait()
    loads[3].wait()
    src = sources[...]
    src = jnp.where(src >= RIM, src - RIM, src + (EXTENT - RIM))
    source_hot = jnp.where(
        lax.broadcasted_iota(jnp.int32, (EXTENT, EDGES), 0) == src, 1.0, 0.0
    ).astype(BF16)
    target_hot = jnp.where(
        lax.broadcasted_iota(jnp.int32, (NODES, EDGES), 0) == targets[...], 1.0, 0.0
    ).astype(BF16)
    count = dot_last(target_hot, source_hot)
    counts[...] = count.astype(BF16)
    inv_s[...] = 1.0 / jnp.maximum(jnp.sum(count, axis=1, keepdims=True), 1.0)
    total[...] = dot(counts[:, pl.ds(0, NODES)], nodes[...])
    loads[5].wait()
    for copy in rim_first:
        copy.wait_recv()
    total[...] += dot(counts[:, pl.ds(NODES, 2 * RIM)], rim_in[...])
    gain_row = gain[...].reshape(1, D)

    def normalize(i, carry):
        at = chunk(i, 32)
        mixed = nodes[at, :].astype(F32) + total[at, :] * inv_s[at, :]
        scaling = lax.rsqrt(jnp.mean(mixed * mixed, axis=1, keepdims=True) + 1e-05)
        scale_s[at, :] = scaling
        norm = mixed * scaling
        normal[at, :] = norm
        dmean[at, :] = (norm * gain_row).astype(BF16)
        return carry

    lax.fori_loop(0, NODES // 32, normalize, 0, unroll=8)
    bucket(dmean, send_r, EARLY)
    exchange(send_r, recv_r, 1, EARLY)
    bucket(dmean, send_r, LATE)
    recv_r[me] = send_r[own]

    def turn(source, out):
        def body(i, carry):
            out[chunk(i, 128), :] = jnp.transpose(source[:, chunk(i, 128)])
            return carry

        lax.fori_loop(0, FF // 128, body, 0)

    loads[6].wait()
    turn(wd, wdt)
    loads[7].wait()
    turn(wg, wgt)
    loads[8].wait()
    turn(wu, wut)

    def flat(ref):
        return ref[...].reshape(ROWS, D)

    def mod(i):
        return lax.rem(i + 2 * REPS, REPS)

    def parts(i):
        low = mod(rep - 1 - i) * SLICE
        high = mod(rep + 1 + i) * SLICE + PART
        return [pl.ds(pl.multiple_of(x, PART), PART) for x in (low, high)]

    def item_rows(i, ref):
        low, high = parts(i)
        return jnp.concatenate([ref[low, :], ref[high, :]], axis=0)

    def hop(d, k, j):
        source = partial.at[0, j, d] if k == 0 else ring.at[k - 1, j, d]
        return pltpu.make_async_remote_copy(
            source, ring.at[k, j, d], ring_send.at[k, j, d], ring_recv.at[k, j, d],
            device_id=(me, rep_up if d == 0 else rep_down), device_id_type=MESH,
        )

    def item_back(i):
        bh_s[...] = dot_last(item_rows(i, wdt), flat(recv_g))

    def item(i, back=True):
        gate_s[...] = dot_last(item_rows(i, wgt), flat(recv_r))
        up_s[...] = dot_last(item_rows(i, wut), flat(recv_r))
        if back:
            item_back(i)
        for d, units in enumerate(parts(i)):

            def act(n, carry):
                rows = pl.ds(pl.multiple_of(d * PART + n * 16, 16), 16)
                here = pl.ds(pl.multiple_of(units.start + n * 16, 16), 16)
                g, u, b = gate_s[rows, :], up_s[rows, :], bh_s[rows, :]
                s = jax.nn.sigmoid(g)
                silu = g * s
                hid_t[here, :] = (silu * u).astype(BF16)
                dgate_t[here, :] = (b * u * s * (1.0 + g * (1.0 - s))).astype(BF16)
                dup_t[here, :] = (b * silu).astype(BF16)
                return carry

            lax.fori_loop(0, PART // 16, act, 0, unroll=6 if i == 0 else 2)
        for j, (left, right) in enumerate(((hid_t, recv_g), (dgate_t, recv_r), (dup_t, recv_r))):
            g = dot(item_rows(i, left), flat(right)).astype(BF16)
            for d in range(2):
                partial[i, j, d] = g[d * PART : (d + 1) * PART, :]
            if i == 0:
                for d in range(2):
                    hop(d, 0, j).start()

    def serve(k, j):
        for d in range(2):
            hop(d, k - 1, j).wait_recv()

            def add(i, carry):
                at = chunk(i, 16)
                ring[k - 1, j, d, at, :] = (
                    ring[k - 1, j, d, at, :].astype(F32) + partial[k, j, d, at, :].astype(F32)
                ).astype(BF16)
                return carry

            lax.fori_loop(0, PART // 16, add, 0, unroll=3)
            hop(d, k, j).start()

    @pl.when(mc == EARLY)
    def _():
        exchange_wait(recv_g, 0)
        item_back(0)

    for slot, source in enumerate((send_g, send_r)):
        exchange_sent(source, slot, EARLY)
    exchange(send_g, recv_g, 0, LATE)
    exchange(send_r, recv_r, 1, LATE)

    @pl.when(mc == LATE)
    def _():
        exchange_wait(recv_g, 0)
        item_back(0)

    exchange_wait(recv_r, 1)
    item(0, back=False)
    item(1)
    serve(1, 0)
    item(2)
    serve(1, 1)
    item(3)
    serve(1, 2)
    serve(2, 0)
    item(4)
    serve(2, 1)
    item(5)
    serve(2, 2)
    serve(3, 0)
    item(6)
    item(7)

    def project(terms, out):
        def body(b, carry):
            at = chunk(b, 256)
            y = dot(terms[0][0][at, :], terms[0][1][...])
            for w, x in terms[1:]:
                y = y + dot(w[at, :], x[...])
            out[:, :, at] = jnp.transpose(y).astype(BF16).reshape(EXPERTS, CAP, 256)
            return carry

        lax.fori_loop(0, D // 256, body, 0)

    project(((wd, hid_t),), back_e)
    for core in range(2):
        exchange(back_e, ret_e, 2, core)
    ret_e[me] = back_e[me]
    serve(3, 1)
    project(((wg, dgate_t), (wu, dup_t)), back_d)
    for core in range(2):
        exchange(back_d, ret_d, 3, core)
    ret_d[me] = back_d[me]
    serve(3, 2)
    serve(4, 0)
    rank_col = jnp.sum(jnp.where(same & (second < first), 1.0, 0.0), axis=1, keepdims=True)
    slot_col = (code_col * CAP + rank_col).astype(jnp.int32)
    place[...] = jnp.where(
        lax.broadcasted_iota(jnp.int32, (NODES, ROWS), 1) == slot_col, 1.0, 0.0
    ).astype(BF16)
    counts_t[...] = jnp.transpose(counts[...].astype(F32)).astype(BF16)
    serve(4, 1)
    serve(4, 2)
    for j in range(3):
        serve(5, j)

    exchange_wait(ret_e, 2)
    total[...] = dot(place[...], flat(ret_e))

    def forward_out(i, carry):
        at = chunk(i, 32)
        layer_out[at, :] = (nodes[at, :].astype(F32) + total[at, :]).astype(BF16)
        return carry

    lax.fori_loop(0, NODES // 32, forward_out, 0)
    exchange_wait(ret_d, 3)
    total[...] = dot(place[...], flat(ret_d))

    def norm_back(i, carry):
        at = chunk(i, 32)
        d_norm = total[at, :] * gain_row
        norm = normal[at, :]
        d_mixed = scale_s[at, :] * (d_norm - norm * jnp.mean(d_norm * norm, axis=1, keepdims=True))
        dmean[at, :] = (d_mixed * inv_s[at, :]).astype(BF16)
        total[at, :] = d_out[at, :].astype(F32) + d_mixed
        return carry

    lax.fori_loop(0, NODES // 32, norm_back, 0, unroll=4)
    rim_out[...] = dot(counts_t[pl.ds(NODES, 2 * RIM), :], dmean[...]).astype(BF16)
    rim_last = rim_copies(rim_out.at[pl.ds(RIM, RIM)], rim_out.at[pl.ds(0, RIM)], rim_back, 2)
    for copy in rim_last:
        copy.start()
    serve(6, 0)
    total[...] += dot(counts_t[pl.ds(0, NODES), :], dmean[...])
    serve(6, 1)
    serve(6, 2)
    for copy in rim_last:
        copy.wait_recv()
    total[pl.ds(0, RIM), :] += rim_back[pl.ds(RIM, RIM), :].astype(F32)
    total[pl.ds(NODES - RIM, RIM), :] += rim_back[pl.ds(0, RIM), :].astype(F32)

    def node_out(i, carry):
        at = chunk(i, 32)
        d_nodes[at, :] = total[at, :].astype(BF16)
        return carry

    lax.fori_loop(0, NODES // 32, node_out, 0)
    for copy in rim_first + rim_last:
        copy.wait_send()
    for slot, source in enumerate((send_g, send_r, back_e, back_d)):
        for core in range(2):
            if slot > 1 or core == LATE:
                exchange_sent(source, slot, core)
        part = source.at[0]
        pltpu.make_async_copy(part, part, a2a_send.at[slot, 2]).wait()
    for k in range(REPS - 2):
        for j in range(3):
            for d in range(2):
                hop(d, k, j).wait_send()

    for j, out in enumerate((grad_down, grad_gate, grad_up)):
        for d in range(2):
            hop(d, 6, j).wait_recv()

            def last(i, carry):
                at = chunk(i, 16)
                out[pl.ds(pl.multiple_of(d * PART + i * 16, 16), 16), :] = (
                    ring[6, j, d, at, :].astype(F32) + partial[7, j, d, at, :].astype(F32)
                )
                return carry

            lax.fori_loop(0, PART // 16, last, 0, unroll=6)
    for j in range(3):
        for d in range(2):
            hop(d, 6, j).wait_send()


def finish(*refs):
    count = (len(refs) - 1) // 2
    copies = [
        pltpu.make_async_copy(refs[i], refs[count + i], refs[-1].at[i]) for i in range(count)
    ]
    for copy in copies:
        copy.start()
    for copy in copies:
        copy.wait()


def on_device(node_feats, edge_src, edge_dst, node_codes, norm_gain, w_gate, w_up, w_down_t, d_out):
    hbm = pl.BlockSpec(memory_space=pl.ANY)
    vmem = pltpu.VMEM
    sem = pltpu.SemaphoreType.DMA
    weight = vmem((D, FF), BF16)
    weight_t = vmem((FF, D), BF16)
    buckets = vmem((EXPERTS, CAP, D), BF16)
    act_t = vmem((FF, ROWS), BF16)
    rows = vmem((NODES, D), BF16)
    wide = vmem((NODES, D), F32)
    item = vmem((SLICE, ROWS), F32)
    rims = vmem((2 * RIM, D), BF16)
    outs = [jax.ShapeDtypeStruct((NODES, D), BF16)] * 2 + [
        jax.ShapeDtypeStruct((SLICE, D), F32)
    ] * 3
    out = pl.pallas_call(
        kernel,
        out_shape=[vmem(x.shape, x.dtype) for x in outs],
        in_specs=[hbm] * 9,
        out_specs=[pl.BlockSpec(memory_space=vmem)] * 5,
        scratch_shapes=[
            rows,
            vmem((1, EDGES), jnp.int32),
            vmem((1, EDGES), jnp.int32),
            vmem((1, NODES), jnp.int32),
            vmem((D,), F32),
            rows,
        ]
        + [weight] * 3
        + [weight_t] * 3
        + [vmem((REPS, 3, 2, PART, D), BF16), vmem((REPS - 1, 3, 2, PART, D), BF16)]
        + [buckets] * 8
        + [act_t] * 3
        + [item] * 3
        + [
            wide,
            wide,
            vmem((NODES, EXTENT), BF16),
            vmem((EXTENT, NODES), BF16),
            vmem((NODES, ROWS), BF16),
            vmem((ROWS, NODES), BF16),
            vmem((NODES, 1), F32),
            vmem((NODES, 1), F32),
        ]
        + [rims] * 3
        + [
            rows,
            sem((9,)),
            sem((4,)),
            sem((4,)),
            sem((4, 3)),
            sem((4,)),
            sem((REPS - 1, 3, 2)),
            sem((REPS - 1, 3, 2)),
        ],
        compiler_params=pltpu.CompilerParams(
            collective_id=0, has_side_effects=True, vmem_limit_bytes=58 * 2**20
        ),
        name="graph_moe",
    )(
        node_feats[0], edge_src, edge_dst, node_codes.reshape(1, NODES), norm_gain,
        w_gate[0], w_up[0], w_down_t[0], d_out[0],
    )
    layer_out, d_nodes, *grads = pl.pallas_call(
        finish,
        out_shape=outs,
        in_specs=[pl.BlockSpec(memory_space=vmem)] * 5,
        out_specs=[hbm] * 5,
        scratch_shapes=[sem((5,))],
        name="results",
    )(*(pltpu.with_memory_space_constraint(x, pltpu.VMEM) for x in out))
    return (layer_out[None], d_nodes[None], *(g.T[None] for g in grads))


def solution(mesh):
    rows = P("rep", "expert", None)
    edges = P("rep", "expert")
    weights = P("expert", None, None)
    grads = P("expert", None, "rep")
    return jax.shard_map(
        on_device,
        mesh=mesh,
        in_specs=(rows, edges, edges, rows, P(), weights, weights, weights, rows),
        out_specs=(rows, rows, grads, grads, grads),
        check_vma=False,
    )
```
